128 devices in a mesh: dp: 16 (over z, y_lo, core), rows: 8 (over x, y_hi).
Axes of the slice: x: 4, y: 4 (y_hi: 2, y_lo: 2; y = y_hi * 2 + y_lo), z: 4, core: 2. Of those that a mesh axis runs over, the one named last changes fastest.
Arguments:
- features: bfloat16 [16, 1, 16, 128, 384], P('dp', None, 'rows'), may hold values from -6 to 6
- past_frames: bfloat16 [16, 2, 16, 128, 384], P('dp', None, 'rows'), may hold values from -6 to 6
- upstream: bfloat16 [16, 1, 16, 128, 384], P('dp', None, 'rows'), may hold values from -6 to 6
- query_weight: bfloat16 [384, 384], replicated, may hold values from -8 to 8
- key_weight: bfloat16 [384, 384], replicated, may hold values from -8 to 8
- value_weight: bfloat16 [384, 384], replicated, may hold values from -0.3125 to 0.3125
- out_weight: bfloat16 [384, 384], replicated, may hold values from -0.3125 to 0.3125
- conv_weight: bfloat16 [384, 27, 384], P(('dp', 'rows')), may hold values from -0.0625 to 0.0625
Outputs:
- feature_grad: bfloat16 [16, 1, 16, 128, 384], P('dp', None, 'rows')
- proj_grads: float32 [384, 1536], P(('dp', 'rows'))
- conv_grad: float32 [384, 10368], P(('dp', 'rows'))
The draws below stay inside these ranges and needn't reach their ends.
All inputs are finite; a program needn't handle non-finite values.
Results may differ from the reference program's by a relative error of at most 0.015.
Values may be sent and summed in bfloat16 or wider, within the bound.
No kernel may reach another device: no remote copies, remote signals or barrier semaphores. Data moves between devices by JAX's collectives and lax.ppermute only.
A program may use at most 128 MiB of HBM per device.

```python
import jax
import jax.numpy as jnp
from jax import lax

C = 384
FRAMES = 1
W = 128
CLIPS = 16
H = 16


def draw_query_weight(key, part):
    key = jax.random.fold_in(key, 11)
    base = jax.random.normal(key, (C, C), jnp.float32) * C ** (-0.5)
    return base.astype(jnp.bfloat16)


def draw_key_weight(key, part):
    key = jax.random.fold_in(key, 12)
    base = jax.random.normal(key, (C, C), jnp.float32) * C ** (-0.5)
    return base.astype(jnp.bfloat16)


def steps_of(own_key, shape, shards, low, largest):
    factor_of, own = 1.0, jax.random.fold_in(own_key, 6)
    for dim, parts in shards:
        heights = jnp.exp(jax.random.uniform(jax.random.fold_in(own, dim), (parts,), jnp.float32, low / len(shards), largest / len(shards)))
        factor_of = factor_of * jnp.repeat(heights, shape[dim] // parts).reshape([-1 if axis == dim else 1 for axis in range(len(shape))])
    return factor_of


def normal_values(stream_key, shape, scale, reach, split=(), held_as=jnp.bfloat16):
    drawn = jax.random.normal(stream_key, shape, jnp.float32) * scale
    if len(split) > 0:
        drawn = steps_of(stream_key, shape, split, -0.22, 0.18) * drawn
    return jnp.clip(drawn, min=-reach, max=reach).astype(held_as)


def setup_inputs(seed: int = 0) -> dict:
    arg_keys = jax.random.split(jax.random.key(seed), 9)
    features = normal_values(arg_keys[0], (CLIPS, FRAMES, H, W, C), 1.0, 6.0, ((0, 16), (2, 8)))
    past_frames = normal_values(arg_keys[1], (CLIPS, 2, H, W, C), 1.0, 6.0, ((0, 16), (2, 8)))
    upstream = normal_values(arg_keys[2], (CLIPS, FRAMES, H, W, C), 1.0, 6.0, ((0, 16), (2, 8)))
    query_weight = draw_query_weight(jax.random.fold_in(arg_keys[8], 71), 0)
    key_weight = draw_key_weight(jax.random.fold_in(arg_keys[8], 71), 0)
    value_weight = normal_values(arg_keys[5], (C, C), C ** -0.5, 0.3125)
    out_weight = normal_values(arg_keys[6], (C, C), C ** -0.5, 0.3125)
    conv_weight = normal_values(arg_keys[7], (C, 27, C), (27 * C) ** -0.5, 0.0625, ((0, 128),))
    return {"features": features, "past_frames": past_frames, "upstream": upstream, "query_weight": query_weight, "key_weight": key_weight, "value_weight": value_weight, "out_weight": out_weight, "conv_weight": conv_weight}


def clip_pass(features, past_frames, upstream, wq, wk, wv, wo, wc):
    frames, height, width, chans = features.shape
    f32 = jnp.float32
    xf = features.astype(f32)
    recip = lax.rsqrt(lax.optimization_barrier(jnp.mean(xf * xf, -1, keepdims=True)) + 1e-06)
    normed = (xf * recip).astype(jnp.bfloat16)
    tokens = normed.reshape(frames, height * width, chans)

    def project(weight):
        return jnp.einsum('ftc,cd->ftd', tokens.astype(f32), weight.astype(f32)).astype(jnp.bfloat16)
    query, key, value = (project(wq), project(wk), project(wv))
    scale = chans ** (-0.5)
    scores = jnp.einsum('fqd,fkd->fqk', query.astype(f32), key.astype(f32)) * scale
    probs = jax.nn.softmax(scores, -1)
    probs_b = probs.astype(jnp.bfloat16)
    attended = jnp.einsum('fqk,fkd->fqd', probs_b.astype(f32), value.astype(f32)).astype(jnp.bfloat16)
    mixed = (xf.reshape(frames, -1, chans) + jnp.einsum('ftd,de->fte', attended.astype(f32), wo.astype(f32))).astype(jnp.bfloat16)
    mixed = mixed.reshape(frames, height, width, chans)
    stacked = jnp.concatenate([past_frames, mixed], 0)
    stack_pad = jnp.pad(stacked, ((0, 0), (1, 1), (1, 1), (0, 0))).astype(f32)
    grad_pad = jnp.pad(upstream, ((0, 2), (1, 1), (1, 1), (0, 0))).astype(f32)
    dz = upstream.astype(f32)
    grad_mixed = jnp.zeros((frames, height, width, chans), f32)
    conv_terms = []
    for tap in range(27):
        t, i, j = (tap // 9, tap // 3 % 3, tap % 3)
        weight = wc[:, tap, :].astype(f32)
        piece = grad_pad[2 - t:2 - t + frames, 2 - i:2 - i + height, 2 - j:2 - j + width]
        grad_mixed = grad_mixed + jnp.einsum('fhwo,io->fhwi', piece, weight)
        inputs = stack_pad[t:t + frames, i:i + height, j:j + width]
        conv_terms.append(jnp.einsum('fhwc,fhwd->cd', inputs, dz))
    conv_term = jnp.stack(conv_terms, 1).reshape(chans, 27 * chans)
    grad_b = grad_mixed.astype(jnp.bfloat16).reshape(frames, -1, chans).astype(f32)
    grad_attended = jnp.einsum('fte,de->ftd', grad_b, wo.astype(f32)).astype(jnp.bfloat16).astype(f32)
    grad_probs = jnp.einsum('fqd,fkd->fqk', grad_attended, value.astype(f32))
    grad_scores = probs * (grad_probs - lax.optimization_barrier(jnp.sum(probs * grad_probs, -1, keepdims=True)))
    scaled = (grad_scores * scale).astype(jnp.bfloat16).astype(f32)
    grad_query = jnp.einsum('fqk,fkd->fqd', scaled, key.astype(f32)).astype(jnp.bfloat16).astype(f32)
    grad_key = jnp.einsum('fqk,fqd->fkd', scaled, query.astype(f32)).astype(jnp.bfloat16).astype(f32)
    grad_value = jnp.einsum('fqk,fqd->fkd', probs_b.astype(f32), grad_attended).astype(jnp.bfloat16).astype(f32)
    tok32 = tokens.astype(f32)
    proj_term = jnp.concatenate([jnp.einsum('ftc,ftd->cd', tok32, grad_query), jnp.einsum('ftc,ftd->cd', tok32, grad_key), jnp.einsum('ftc,ftd->cd', tok32, grad_value), jnp.einsum('ftc,ftd->cd', attended.astype(f32), grad_b)], 1)
    grad_normed = jnp.einsum('ftd,cd->ftc', grad_query, wq.astype(f32)) + jnp.einsum('ftd,cd->ftc', grad_key, wk.astype(f32)) + jnp.einsum('ftd,cd->ftc', grad_value, wv.astype(f32))
    grad_normed = grad_normed.reshape(frames, height, width, chans)
    inner = lax.optimization_barrier(jnp.mean(grad_normed * xf, -1, keepdims=True))
    feature_grad = grad_mixed + recip * grad_normed - xf * recip ** 3 * inner
    return (feature_grad.astype(jnp.bfloat16), proj_term, conv_term)

def reference(features, past_frames, upstream, query_weight, key_weight, value_weight, out_weight, conv_weight):
    chans = features.shape[-1]

    def step(carry, item):
        feats, past, grad = item
        dx, proj_term, conv_term = clip_pass(feats, past, grad, query_weight, key_weight, value_weight, out_weight, conv_weight)
        return ((carry[0] + proj_term, carry[1] + conv_term), dx)
    init = (jnp.zeros((chans, 4 * chans), jnp.float32), jnp.zeros((chans, 27 * chans), jnp.float32))
    (proj_grads, conv_grad), feature_grad = lax.scan(step, init, (features, past_frames, upstream))
    return (feature_grad, proj_grads, conv_grad)
```

```python
import jax
import jax.numpy as jnp
import numpy as np
from jax import lax
from jax.experimental import pallas as pl
from jax.experimental.pallas import tpu as pltpu
from jax.sharding import PartitionSpec as P

F32 = jnp.float32
BF16 = jnp.bfloat16
VMEM_BYTES = 56 * 1024 * 1024


def nn(a, b):
    return lax.dot_general(a, b, (((1,), (0,)), ((), ())), preferred_element_type=F32)


def nt(a, b):
    return lax.dot_general(a, b, (((1,), (1,)), ((), ())), preferred_element_type=F32)


def whole(count):
    return [pl.BlockSpec(memory_space=pltpu.VMEM)] * count


def params():
    return pltpu.CompilerParams(vmem_limit_bytes=VMEM_BYTES)


def cost(macs, size):
    return pl.CostEstimate(flops=2 * macs, bytes_accessed=size, transcendentals=0)


def eye_of(n):
    rows = lax.broadcasted_iota(jnp.int32, (n, n), 0)
    cols = lax.broadcasted_iota(jnp.int32, (n, n), 1)
    return jnp.where(rows == cols, 1.0, 0.0).astype(BF16)


def pack_kernel(x_ref, u_ref, past_ref, order_ref, out_ref):
    chans, cells = x_ref.shape[1], x_ref.shape[0]
    groups = out_ref.shape[0]
    part = chans // groups
    eye = eye_of(chans)
    x_t = nt(eye, x_ref[...]).astype(BF16)
    u_t = nt(eye, u_ref[...]).astype(BF16)
    for r in range(groups):
        out_ref[r, 0:chans, :] = x_t
        out_ref[r, chans : 2 * chans, :] = u_t
    for f in range(2):
        p_t = nt(order_ref[...], past_ref[f]).astype(BF16)
        for r in range(groups):
            at = 2 * chans + f * part
            out_ref[r, at : at + part, :] = p_t[r * part : (r + 1) * part]


def conv_input_kernel(width, got_ref, w_ref, out_ref, wide_ref, w32_ref, wcat_ref):
    groups = got_ref.shape[0]
    cells = got_ref.shape[2]
    part, total = out_ref.shape
    chans = w_ref.shape[2]
    slots, padded = w_ref.shape[0], w_ref.shape[1]
    per = part // slots
    for c in range(chans // 128):
        lanes = slice(c * 128, (c + 1) * 128)
        for d in range(slots):
            w32_ref[c, d * padded : (d + 1) * padded, :] = w_ref[d, :, lanes].astype(F32)
        for tap in range(9):
            for k in range(per):
                rows = w32_ref[c, pl.ds(k * 9 + tap, slots, stride=padded), :]
                at = tap * part + k * slots
                wcat_ref[at : at + slots, lanes] = rows.astype(BF16)
    wide_ref[:, 0:width] = jnp.zeros((9 * part, width), F32)
    wide_ref[:, width + total :] = jnp.zeros((9 * part, width), F32)
    for r in range(groups):
        wide_ref[:, width + r * cells : width + (r + 1) * cells] = nn(
            wcat_ref[...], got_ref[r, chans : 2 * chans, :]
        )
    lane = lax.broadcasted_iota(jnp.int32, (part, total), 1) % width
    sums = []
    for j in range(3):
        piece = None
        for i in range(3):
            tap = 3 * i + j
            at = (2 - i) * width
            term = wide_ref[tap * part : (tap + 1) * part, at : at + total]
            piece = term if piece is None else piece + term
        sums.append(piece)
    first = jnp.where(lane == width - 1, 0.0, pltpu.roll(sums[0], total - 1, 1))
    last = jnp.where(lane == 0, 0.0, pltpu.roll(sums[2], 1, 1))
    out_ref[...] = (first + sums[1] + last).astype(BF16)


def forward_kernel(
    width,
    got_ref,
    wq_ref,
    wk_ref,
    wv_ref,
    wo_ref,
    pick_ref,
    qt_ref,
    kt_ref,
    key_ref,
    value_ref,
    att_ref,
    top_ref,
    inv_ref,
    terms_ref,
    vt_ref,
    side_ref,
    ut_ref,
    acc_ref,
):
    groups, cells = got_ref.shape[0], got_ref.shape[2]
    chans = wq_ref.shape[0]
    total = groups * cells
    part = pick_ref.shape[0]
    scale = chans ** (-0.5)
    eye = eye_of(chans)
    eye_cells = eye_of(cells)
    wq_t = nt(eye, wq_ref[...]).astype(BF16)
    wk_t = nt(eye, wk_ref[...]).astype(BF16)
    wv_t = nt(eye, wv_ref[...]).astype(BF16)
    wo_t = nt(eye, wo_ref[...]).astype(BF16)
    wo_pick = nn(pick_ref[...], wo_t).astype(BF16)

    def project(r, carry):
        x = got_ref[r, 0:chans, :].astype(F32)
        recip = lax.rsqrt(jnp.mean(x * x, 0, keepdims=True) + 1e-06)
        normed = (x * recip).astype(BF16)
        qt_ref[r] = nn(wq_t, normed).astype(BF16)
        k_t = nn(wk_t, normed).astype(BF16)
        kt_ref[r] = k_t
        v_t = nn(wv_t, normed).astype(BF16)
        vt_ref[r] = v_t
        at = pl.ds(pl.multiple_of(r * cells, cells), cells)
        key_ref[at, :] = nt(eye_cells, k_t).astype(BF16)
        value_ref[at, :] = nt(eye_cells, v_t).astype(BF16)
        return carry

    lax.fori_loop(0, groups, project, 0)
    for r in range(groups):
        ut_ref[:, r * cells : (r + 1) * cells] = got_ref[r, chans : 2 * chans, :]

    for n in range(9):
        rows = slice(n * part, (n + 1) * part)
        side_ref[rows, 0:width] = jnp.zeros((part, width), BF16)
        side_ref[rows, width + total :] = jnp.zeros((part, width), BF16)

    lane = lax.broadcasted_iota(jnp.int32, (part, cells), 1) % width

    def place(t, r, block):
        at = pl.ds(pl.multiple_of(width + r * cells, width), cells)
        block32 = block.astype(F32)
        left = jnp.where(lane == 0, 0.0, pltpu.roll(block32, 1, 1))
        right = jnp.where(lane == width - 1, 0.0, pltpu.roll(block32, cells - 1, 1))
        side_ref[(3 * t) * part : (3 * t + 1) * part, at] = left.astype(BF16)
        side_ref[(3 * t + 1) * part : (3 * t + 2) * part, at] = block
        side_ref[(3 * t + 2) * part : (3 * t + 3) * part, at] = right.astype(BF16)

    def attend(r, carry):
        scores = nn(key_ref[...], qt_ref[r]) * scale
        top = jnp.max(scores, 0, keepdims=True)
        raised = jnp.exp(scores - top)
        inv = 1.0 / jnp.sum(raised, 0, keepdims=True)
        raised_b = raised.astype(BF16)
        att = jnp.zeros((chans, cells), F32)
        for b in range(groups):
            att = att + nn(vt_ref[b], raised_b[b * cells : (b + 1) * cells])
        att = att * inv
        att_ref[r] = att
        top_ref[r] = top
        inv_ref[r] = inv
        x_pick = nn(pick_ref[...], got_ref[r, 0:chans, :])
        mixed = (x_pick + nn(wo_pick, att.astype(BF16))).astype(BF16)
        place(2, r, mixed)
        for f in range(2):
            place(f, r, got_ref[r, 2 * chans + f * part : 2 * chans + (f + 1) * part, :])
        return carry

    lax.fori_loop(0, groups, attend, 0)

    lane_tiles = chans // 128
    acc_ref[:, 27 * part :, :] = jnp.zeros((lane_tiles, 5 * part, 128), F32)
    for i in range(3):
        block = nt(side_ref[:, i * width : i * width + total], ut_ref[...])
        for t in range(3):
            for j in range(3):
                tap, at = 9 * t + 3 * i + j, (3 * t + j) * part
                for c in range(lane_tiles):
                    acc_ref[c, tap * part : (tap + 1) * part, :] = block[
                        at : at + part, c * 128 : (c + 1) * 128
                    ]
    slots = terms_ref.shape[0]
    for d in range(slots):
        for k in range(part // slots):
            for c in range(lane_tiles):
                rows = acc_ref[c, pl.ds(k * slots + d, 32, stride=part), :]
                terms_ref[d, k * 32 : (k + 1) * 32, c * 128 : (c + 1) * 128] = rows.astype(BF16)


def backward_kernel(
    me_ref,
    got_ref,
    grad_ref,
    qt_ref,
    kt_ref,
    key_ref,
    value_ref,
    att_ref,
    top_ref,
    inv_ref,
    wq_ref,
    wk_ref,
    wv_ref,
    wo_ref,
    order_ref,
    back_ref,
    out_ref,
    terms_ref,
    ga_ref,
    tot_ref,
    gq_ref,
    gk_ref,
    gv_ref,
):
    groups, cells = got_ref.shape[0], got_ref.shape[2]
    chans = wq_ref.shape[0]
    scale = chans ** (-0.5)
    me = me_ref[0]
    wo_order = nt(wo_ref[...], order_ref[...]).astype(BF16)

    def spread(r, carry):
        at = pl.ds(pl.multiple_of(r * cells, cells), cells)
        ga = nn(wo_order, grad_ref[:, at]).astype(BF16)
        ga_ref[r] = ga
        tot_ref[r] = jnp.sum(att_ref[r] * ga.astype(F32), 0, keepdims=True)
        return carry

    lax.fori_loop(0, groups, spread, 0)

    mine = pl.ds(pl.multiple_of(me * cells, cells), cells)
    key_mine = key_ref[mine, :]
    value_mine = value_ref[mine, :]
    q_mine = qt_ref[me]
    ga_mine = ga_ref[me]
    top_mine = top_ref[me]
    inv_mine = inv_ref[me]
    tot_mine = tot_ref[me]
    gq_ref[...] = jnp.zeros((chans, cells), F32)
    gk_ref[...] = jnp.zeros((chans, cells), F32)
    gv_ref[...] = jnp.zeros((chans, cells), F32)

    def step(r, carry):
        at = pl.ds(pl.multiple_of(r * cells, cells), cells)
        probs = jnp.exp(nn(key_ref[at, :], q_mine) * scale - top_mine) * inv_mine
        grad_probs = nn(value_ref[at, :], ga_mine)
        scaled = (probs * (grad_probs - tot_mine) * scale).astype(BF16)
        gq_ref[...] += nn(kt_ref[r], scaled)
        probs = jnp.exp(nn(key_mine, qt_ref[r]) * scale - top_ref[r]) * inv_ref[r]
        grad_probs = nn(value_mine, ga_ref[r])
        scaled = (probs * (grad_probs - tot_ref[r]) * scale).astype(BF16)
        gk_ref[...] += nt(qt_ref[r], scaled)
        gv_ref[...] += nt(ga_ref[r], probs.astype(BF16))
        return carry

    lax.fori_loop(0, groups, step, 0)

    gq = gq_ref[...].astype(BF16)
    gk = gk_ref[...].astype(BF16)
    gv = gv_ref[...].astype(BF16)
    x = got_ref[me, 0:chans, :].astype(F32)
    recip = lax.rsqrt(jnp.mean(x * x, 0, keepdims=True) + 1e-06)
    normed = (x * recip).astype(BF16)
    grad_b = nn(back_ref[...], grad_ref[:, mine])
    grad_normed = nn(wq_ref[...], gq) + nn(wk_ref[...], gk) + nn(wv_ref[...], gv)
    inner = jnp.mean(grad_normed * x, 0, keepdims=True)
    out = grad_b + recip * grad_normed - x * (recip * recip * recip) * inner
    out_ref[...] = nt(eye_of(cells), out.astype(BF16)).astype(BF16)
    slots = terms_ref.shape[0]
    each = chans // slots
    pairs = [(normed, gq), (normed, gk), (normed, gv), (att_ref[me].astype(BF16), grad_b.astype(BF16))]
    for n, (left, right) in enumerate(pairs):
        term = nt(left, right).astype(BF16)
        for d in range(slots):
            terms_ref[d, n * each : (n + 1) * each, :] = term[d * each : (d + 1) * each]


def spread_over(block, axis):
    count = lax.axis_size(axis)
    return lax.all_to_all(jnp.broadcast_to(block[None], (count, *block.shape)), axis, 0, 0)


def shards(
    features, past_frames, upstream, query_weight, key_weight, value_weight, out_weight, conv_weight
):
    slots, groups = lax.axis_size("dp"), lax.axis_size("rows")
    _, _, rows_here, width, chans = features.shape
    cells = rows_here * width
    total = cells * groups
    part = chans // groups
    per = part // slots
    me = lax.axis_index("rows")

    order = np.zeros((chans, chans), np.float32)
    for r in range(groups):
        for k in range(per):
            for d in range(slots):
                order[r * part + k * slots + d, d * per * groups + per * r + k] = 1.0
    order_b = jnp.asarray(order, BF16)
    back_b = jnp.asarray(order.T, BF16)
    pick = lax.dynamic_slice_in_dim(order_b, me * part, part, axis=0)

    x = features.reshape(cells, chans)
    u = upstream.reshape(cells, chans)
    past = past_frames.reshape(2, cells, chans)
    depth = 2 * chans + 2 * part
    packed = pl.pallas_call(
        pack_kernel,
        out_shape=jax.ShapeDtypeStruct((groups, depth, cells), BF16),
        in_specs=whole(4),
        out_specs=pl.BlockSpec(memory_space=pltpu.VMEM),
        compiler_params=params(),
        name="pack",
    )(x, u, past, order_b)
    got = lax.all_to_all(packed, "rows", 0, 0)

    w_local = conv_weight[:, 18:27, :].reshape(per * 9, chans)
    w_local = jnp.pad(w_local, ((0, 32 - per * 9), (0, 0)))
    w_all = spread_over(w_local, "dp")

    grad_part = pl.pallas_call(
        lambda *refs: conv_input_kernel(width, *refs),
        out_shape=jax.ShapeDtypeStruct((part, total), BF16),
        in_specs=whole(2),
        out_specs=pl.BlockSpec(memory_space=pltpu.VMEM),
        scratch_shapes=[
            pltpu.VMEM((9 * part, total + 2 * width), F32),
            pltpu.VMEM((chans // 128, slots * 32, 128), F32),
            pltpu.VMEM((9 * part, chans), BF16),
        ],
        compiler_params=params(),
        name="conv_input",
    )(got, w_all)
    grad_all = spread_over(grad_part, "rows").reshape(chans, total)

    qt, kt, key, value, att, top, inv, conv_terms = pl.pallas_call(
        lambda *refs: forward_kernel(width, *refs),
        out_shape=(
            jax.ShapeDtypeStruct((groups, chans, cells), BF16),
            jax.ShapeDtypeStruct((groups, chans, cells), BF16),
            jax.ShapeDtypeStruct((total, chans), BF16),
            jax.ShapeDtypeStruct((total, chans), BF16),
            jax.ShapeDtypeStruct((groups, chans, cells), F32),
            jax.ShapeDtypeStruct((groups, 1, cells), F32),
            jax.ShapeDtypeStruct((groups, 1, cells), F32),
            jax.ShapeDtypeStruct((slots, per * 32, chans), BF16),
        ),
        in_specs=whole(6),
        out_specs=tuple(whole(8)),
        scratch_shapes=[
            pltpu.VMEM((groups, chans, cells), BF16),
            pltpu.VMEM((9 * part, total + 2 * width), BF16),
            pltpu.VMEM((chans, total), BF16),
            pltpu.VMEM((chans // 128, 32 * part, 128), F32),
        ],
        compiler_params=params(),
        name="forward",
    )(got, query_weight, key_weight, value_weight, out_weight, pick)

    feature_grad, proj_terms = pl.pallas_call(
        backward_kernel,
        out_shape=(
            jax.ShapeDtypeStruct((cells, chans), BF16),
            jax.ShapeDtypeStruct((slots, 4 * chans // slots, chans), BF16),
        ),
        in_specs=[pl.BlockSpec(memory_space=pltpu.SMEM)] + whole(15),
        out_specs=tuple(whole(2)),
        scratch_shapes=[
            pltpu.VMEM((groups, chans, cells), BF16),
            pltpu.VMEM((groups, 1, cells), F32),
            pltpu.VMEM((chans, cells), F32),
            pltpu.VMEM((chans, cells), F32),
            pltpu.VMEM((chans, cells), F32),
        ],
        compiler_params=params(),
        name="backward",
    )(
        me.reshape(1),
        got,
        grad_all,
        qt,
        kt,
        key,
        value,
        att,
        top,
        inv,
        query_weight,
        key_weight,
        value_weight,
        out_weight,
        order_b,
        back_b,
    )

    conv_sum = jnp.sum(lax.all_to_all(conv_terms, "dp", 0, 0).astype(F32), 0)
    conv_grad = conv_sum.reshape(per, 32, chans)[:, :27].reshape(per, 27 * chans)
    proj_sum = jnp.sum(lax.all_to_all(proj_terms, "dp", 0, 0).astype(F32), 0)
    proj_sum = proj_sum.reshape(4, groups, per, chans).transpose(1, 2, 0, 3)
    proj_sum = proj_sum.reshape(groups, per, 4 * chans)
    proj_grads = jnp.sum(lax.all_to_all(proj_sum, "rows", 0, 0), 0)
    return feature_grad.reshape(features.shape), proj_grads, conv_grad


def solution(mesh):
    placed = (
        P("dp", None, "rows", None, None),
        P("dp", None, "rows", None, None),
        P("dp", None, "rows", None, None),
        P(),
        P(),
        P(),
        P(),
        P(("dp", "rows"), None, None),
    )
    return jax.shard_map(
        shards,
        mesh=mesh,
        in_specs=placed,
        out_specs=(
            P("dp", None, "rows", None, None),
            P(("dp", "rows"), None),
            P(("dp", "rows"), None),
        ),
        check_vma=False,
    )
```

```python
import jax
import jax.numpy as jnp
import numpy as np
from jax import lax
from jax.experimental import pallas as pl
from jax.experimental.pallas import tpu as pltpu
from jax.sharding import PartitionSpec as P

F32 = jnp.float32
BF16 = jnp.bfloat16
LOG2E = 1.4426950408889634
VMEM_BYTES = 56 * 1024 * 1024


def nn(a, b):
    return lax.dot_general(a, b, (((1,), (0,)), ((), ())), preferred_element_type=F32)


def nt(a, b):
    return lax.dot_general(a, b, (((1,), (1,)), ((), ())), preferred_element_type=F32)


def whole(count):
    return [pl.BlockSpec(memory_space=pltpu.VMEM)] * count


def params():
    return pltpu.CompilerParams(vmem_limit_bytes=VMEM_BYTES)


def cost(macs, size):
    return pl.CostEstimate(flops=2 * macs, bytes_accessed=size, transcendentals=0)


def eye_of(n):
    rows = lax.broadcasted_iota(jnp.int32, (n, n), 0)
    cols = lax.broadcasted_iota(jnp.int32, (n, n), 1)
    return jnp.where(rows == cols, 1.0, 0.0).astype(BF16)


def pack_kernel(x_ref, u_ref, past_ref, order_ref, out_ref):
    chans = x_ref.shape[1]
    groups = out_ref.shape[0]
    part = chans // groups
    eye = eye_of(chans)
    x_t = nt(eye, x_ref[...]).astype(BF16)
    u_t = nt(eye, u_ref[...]).astype(BF16)
    for r in range(groups):
        out_ref[r, 0:chans, :] = x_t
        out_ref[r, chans : 2 * chans, :] = u_t
    for f in range(2):
        p_t = nt(order_ref[...], past_ref[f]).astype(BF16)
        for r in range(groups):
            at = 2 * chans + f * part
            out_ref[r, at : at + part, :] = p_t[r * part : (r + 1) * part]


def conv_input_kernel(width, me_ref, got_ref, w0_ref, w1_ref, w2_ref, w3_ref, out_ref, wide_ref, w32_ref, wcat_ref):
    groups = got_ref.shape[0]
    cells = got_ref.shape[2]
    part, total = out_ref.shape[1:]
    w_refs = (w0_ref, w1_ref, w2_ref, w3_ref)
    near, padded, chans = w0_ref.shape
    slots = 4 * near
    per = part // slots
    me = me_ref[0]
    for back in range(4):
        for n in range(near):
            plane = lax.rem(lax.div(me, near) + 4 - back, 4)
            inner = lax.rem(me, near)
            apart = [(inner // 2 + n // 2) % 2, (inner + n) % 2]
            at = (plane * near + apart[0] * 2 + apart[1]) * padded
            at = pl.ds(pl.multiple_of(at, padded), padded)
            for c in range(chans // 128):
                w32_ref[c, at, :] = w_refs[back][n, :, c * 128 : (c + 1) * 128].astype(F32)
    for c in range(chans // 128):
        lanes = slice(c * 128, (c + 1) * 128)
        for tap in range(9):
            for k in range(per):
                rows = w32_ref[c, pl.ds(k * 9 + tap, slots, stride=padded), :]
                at = tap * part + k * slots
                wcat_ref[at : at + slots, lanes] = rows.astype(BF16)
    wide_ref[:, 0:width] = jnp.zeros((9 * part, width), F32)
    wide_ref[:, width + total :] = jnp.zeros((9 * part, width), F32)
    for r in range(groups):
        wide_ref[:, width + r * cells : width + (r + 1) * cells] = nn(
            wcat_ref[...], got_ref[r, chans : 2 * chans, :]
        )
    lane = lax.broadcasted_iota(jnp.int32, (part, total), 1) % width
    sums = []
    for j in range(3):
        piece = None
        for i in range(3):
            tap = 3 * i + j
            at = (2 - i) * width
            term = wide_ref[tap * part : (tap + 1) * part, at : at + total]
            piece = term if piece is None else piece + term
        sums.append(piece)
    first = jnp.where(lane == width - 1, 0.0, pltpu.roll(sums[0], total - 1, 1))
    last = jnp.where(lane == 0, 0.0, pltpu.roll(sums[2], 1, 1))
    grad = (first + sums[1] + last).astype(BF16)
    for r in range(groups):
        out_ref[r] = grad


def forward_kernel(
    width,
    me_ref,
    got_ref,
    wq_ref,
    wk_ref,
    wv_ref,
    wo_ref,
    order_ref,
    qt_ref,
    kt_ref,
    key_ref,
    value_ref,
    att_ref,
    top_ref,
    inv_ref,
    terms_ref,
    vt_ref,
    side_ref,
    ut_ref,
    acc_ref,
    even_ref,
    odd_ref,
    raised_ref,
):
    groups, cells = got_ref.shape[0], got_ref.shape[2]
    chans = wq_ref.shape[0]
    total = groups * cells
    part = chans // groups
    pick = order_ref[pl.ds(pl.multiple_of(me_ref[0] * part, part), part), :]
    scale = chans ** (-0.5)
    eye = eye_of(chans)
    eye_cells = eye_of(cells)
    wqkv_t = jnp.concatenate(
        [nt(eye, ref[...]).astype(BF16) for ref in (wq_ref, wk_ref, wv_ref)], 0
    )
    wkv = jnp.concatenate([wk_ref[...], wv_ref[...]], 1)
    wo_t = nt(eye, wo_ref[...]).astype(BF16)
    wo_pick = nn(pick, wo_t).astype(BF16)

    def project(r, carry):
        x = got_ref[r, 0:chans, :].astype(F32)
        recip = lax.rsqrt(jnp.mean(x * x, 0, keepdims=True) + 1e-06)
        normed = (x * recip).astype(BF16)
        at = pl.ds(pl.multiple_of(r * cells, cells), cells)
        qkv_t = nn(wqkv_t, normed).astype(BF16)
        qt_ref[:, at] = qkv_t[0:chans]
        kt_ref[:, at] = qkv_t[chans : 2 * chans]
        vt_ref[:, at] = qkv_t[2 * chans :]
        kv = nn(nt(eye_cells, normed).astype(BF16), wkv).astype(BF16)
        key_ref[at, :] = kv[:, 0:chans]
        value_ref[at, :] = kv[:, chans:]
        return carry

    lax.fori_loop(0, groups, project, 0, unroll=2)
    for r in range(groups):
        ut_ref[:, r * cells : (r + 1) * cells] = got_ref[r, chans : 2 * chans, :]

    for n in range(9):
        rows = slice(n * part, (n + 1) * part)
        side_ref[rows, 0:width] = jnp.zeros((part, width), BF16)
        side_ref[rows, width + total :] = jnp.zeros((part, width), BF16)

    lane = lax.broadcasted_iota(jnp.int32, (part, cells), 1) % width

    def place(t, r, block):
        at = pl.ds(pl.multiple_of(width + r * cells, width), cells)
        block32 = block.astype(F32)
        left = jnp.where(lane == 0, 0.0, pltpu.roll(block32, 1, 1))
        right = jnp.where(lane == width - 1, 0.0, pltpu.roll(block32, cells - 1, 1))
        side_ref[(3 * t) * part : (3 * t + 1) * part, at] = left.astype(BF16)
        side_ref[(3 * t + 1) * part : (3 * t + 2) * part, at] = block
        side_ref[(3 * t + 2) * part : (3 * t + 3) * part, at] = right.astype(BF16)

    even_ref[...] = nn(key_ref[...], qt_ref[:, 0:cells])
    chunk = total // 4

    def attend(r, now_ref, later_ref):
        later = jnp.minimum(r + 1, groups - 1)
        at = pl.ds(pl.multiple_of(r * cells, cells), cells)
        later = pl.ds(pl.multiple_of(later * cells, cells), cells)
        top = jnp.max(now_ref[...], 0, keepdims=True)
        count = jnp.zeros((1, cells), F32)
        for b in range(4):
            rows = slice(b * chunk, (b + 1) * chunk)
            later_ref[rows] = nn(key_ref[rows], qt_ref[:, later])
            raised = jnp.exp2((now_ref[rows] - top) * (scale * LOG2E))
            count = count + jnp.sum(raised, 0, keepdims=True)
            raised_ref[rows] = raised.astype(BF16)
        inv = 1.0 / count
        att = nn(vt_ref[...], raised_ref[...]) * inv
        att_ref[:, at] = att
        top_ref[:, at] = top
        inv_ref[:, at] = inv
        x_pick = nn(pick, got_ref[r, 0:chans, :])
        mixed = (x_pick + nn(wo_pick, att.astype(BF16))).astype(BF16)
        place(2, r, mixed)
        for f in range(2):
            place(f, r, got_ref[r, 2 * chans + f * part : 2 * chans + (f + 1) * part, :])

    def attend_two(n, carry):
        attend(2 * n, even_ref, odd_ref)
        attend(2 * n + 1, odd_ref, even_ref)
        return carry

    lax.fori_loop(0, groups // 2, attend_two, 0)

    lane_tiles = chans // 128
    acc_ref[:, 27 * part :, :] = jnp.zeros((lane_tiles, 5 * part, 128), F32)
    for i in range(3):
        block = nt(side_ref[:, i * width : i * width + total], ut_ref[...])
        for t in range(3):
            for j in range(3):
                tap, at = 9 * t + 3 * i + j, (3 * t + j) * part
                for c in range(lane_tiles):
                    acc_ref[c, tap * part : (tap + 1) * part, :] = block[
                        at : at + part, c * 128 : (c + 1) * 128
                    ]
    slots = terms_ref.shape[0]
    for d in range(slots):
        for k in range(part // slots):
            for c in range(lane_tiles):
                rows = acc_ref[c, pl.ds(k * slots + d, 32, stride=part), :]
                terms_ref[d, k * 32 : (k + 1) * 32, c * 128 : (c + 1) * 128] = rows.astype(BF16)


def backward_kernel(
    place_ref,
    x_ref,
    grad_ref,
    qt_ref,
    kt_ref,
    key_ref,
    value_ref,
    att_ref,
    top_ref,
    inv_ref,
    wq_ref,
    wk_ref,
    wv_ref,
    wo_ref,
    order_ref,
    back_ref,
    rows_ref,
    out_ref,
    give_ref,
    keep_ref,
    ga_ref,
    tot_ref,
    sq_ref,
    sk_ref,
    pb_ref,
):
    cells = x_ref.shape[0]
    chans, total = qt_ref.shape
    scale = chans ** (-0.5)
    mine = pl.ds(pl.multiple_of(place_ref[0] * cells, cells), cells)
    core = place_ref[1]
    wo_order = nt(wo_ref[...], order_ref[...]).astype(BF16)
    chunk = total // 4
    chunks = [slice(b * chunk, (b + 1) * chunk) for b in range(4)]
    for at in chunks:
        ga = nn(wo_order, grad_ref[:, at]).astype(BF16)
        ga_ref[:, at] = ga
        tot_ref[:, at] = jnp.sum(att_ref[:, at] * ga.astype(F32), 0, keepdims=True)

    key_mine = key_ref[mine, :]
    value_mine = value_ref[mine, :]
    q_mine = qt_ref[:, mine]
    ga_mine = ga_ref[:, mine]
    top_mine = top_ref[:, mine]
    inv_mine = inv_ref[:, mine]
    tot_mine = tot_ref[:, mine]

    def probs_of(scores, top, inv):
        return jnp.exp2((scores - top) * (scale * LOG2E)) * inv

    for at in chunks:
        probs = probs_of(nn(key_ref[at, :], q_mine), top_mine, inv_mine)
        grad_probs = nn(value_ref[at, :], ga_mine)
        sq_ref[at, :] = (probs * (grad_probs - tot_mine) * scale).astype(BF16)
        probs = probs_of(nn(key_mine, qt_ref[:, at]), top_ref[:, at], inv_ref[:, at])
        grad_probs = nn(value_mine, ga_ref[:, at])
        pb_ref[:, at] = probs.astype(BF16)
        sk_ref[:, at] = (probs * (grad_probs - tot_ref[:, at]) * scale).astype(BF16)

    gq = nn(kt_ref[...], sq_ref[...]).astype(BF16)
    gk = nt(qt_ref[...], sk_ref[...]).astype(BF16)
    gv = nt(ga_ref[...], pb_ref[...]).astype(BF16)
    x = nt(eye_of(chans), x_ref[...])
    recip = lax.rsqrt(jnp.mean(x * x, 0, keepdims=True) + 1e-06)
    normed = (x * recip).astype(BF16)
    grad_b = nn(back_ref[...], grad_ref[:, mine])
    grad_normed = nn(wq_ref[...], gq) + nn(wk_ref[...], gk) + nn(wv_ref[...], gv)
    inner = jnp.mean(grad_normed * x, 0, keepdims=True)
    out = grad_b + recip * grad_normed - x * (recip * recip * recip) * inner
    out_ref[...] = nt(eye_of(cells), out.astype(BF16)).astype(BF16)
    att = att_ref[:, mine].astype(BF16)
    gq_gv = jnp.concatenate([nt(eye_of(cells), gq), nt(eye_of(cells), gv)], 0).astype(BF16)
    gk_gb = jnp.concatenate(
        [nt(eye_of(cells), gk), nt(eye_of(cells), grad_b.astype(BF16))], 0
    ).astype(BF16)
    for half, to_ref in ((1 - core, give_ref), (core, keep_ref)):
        upper = nn(rows_ref[half, 0], normed).astype(BF16)
        lower = nn(rows_ref[half, 1], normed).astype(BF16)
        lower_att = nn(rows_ref[half, 1], att).astype(BF16)
        to_ref[:, 0:chans] = nn(jnp.concatenate([upper, lower], 1), gq_gv).astype(BF16)
        to_ref[:, chans:] = nn(jnp.concatenate([upper, lower_att], 1), gk_gb).astype(BF16)


def shards(
    features, past_frames, upstream, query_weight, key_weight, value_weight, out_weight, conv_weight
):
    slots, groups = lax.axis_size("dp"), lax.axis_size("rows")
    _, _, rows_here, width, chans = features.shape
    cells = rows_here * width
    total = cells * groups
    part = chans // groups
    per = part // slots
    me = lax.axis_index("rows")

    order = np.zeros((chans, chans), np.float32)
    for r in range(groups):
        for k in range(per):
            for d in range(slots):
                order[r * part + k * slots + d, d * per * groups + per * r + k] = 1.0
    order_b = jnp.asarray(order, BF16)
    back_b = jnp.asarray(order.T, BF16)

    pairs = slots // 2
    by_core = np.zeros((2, 2, pairs * groups * 8, chans), np.float32)
    for core in range(2):
        for pair in range(pairs):
            for r in range(groups):
                for k in range(per):
                    row = (pair * groups + r) * 8 + k
                    chan = (2 * pair + core) * per * groups + per * r + k
                    by_core[core, 0, row, chan] = 1.0
                    by_core[core, 1, row + 4, chan] = 1.0
    by_core = jnp.asarray(by_core, BF16)
    core = lax.rem(lax.axis_index("dp"), 2)

    x = features.reshape(cells, chans)
    u = upstream.reshape(cells, chans)
    past = past_frames.reshape(2, cells, chans)
    packed = pl.pallas_call(
        pack_kernel,
        out_shape=jax.ShapeDtypeStruct((groups, 2 * chans + 2 * part, cells), BF16),
        in_specs=whole(4),
        out_specs=pl.BlockSpec(memory_space=pltpu.VMEM),
        compiler_params=params(),
        name="pack",
    )(x, u, past, order_b)
    got = lax.all_to_all(packed, "rows", 0, 0)

    w_local = conv_weight[:, 18:27, :].reshape(per * 9, chans)
    w_local = jnp.pad(w_local, ((0, 32 - per * 9), (0, 0)))
    w_local, packed = lax.optimization_barrier((w_local, packed))
    w_near = w_local[None]
    w_near = jnp.concatenate([w_near, lax.ppermute(w_near, "dp", [(d, d ^ 1) for d in range(slots)])], 0)
    w_near = jnp.concatenate([w_near, lax.ppermute(w_near, "dp", [(d, d ^ 2) for d in range(slots)])], 0)
    w_all = [w_near]
    for back in (1, 2, 3):
        w_all.append(lax.ppermute(w_near, "dp", [(d, (d + 4 * back) % slots) for d in range(slots)]))

    grad_sent = pl.pallas_call(
        lambda *refs: conv_input_kernel(width, *refs),
        out_shape=jax.ShapeDtypeStruct((groups, part, total), BF16),
        in_specs=[pl.BlockSpec(memory_space=pltpu.SMEM)] + whole(5),
        out_specs=pl.BlockSpec(memory_space=pltpu.VMEM),
        scratch_shapes=[
            pltpu.VMEM((9 * part, total + 2 * width), F32),
            pltpu.VMEM((chans // 128, slots * 32, 128), F32),
            pltpu.VMEM((9 * part, chans), BF16),
        ],
        compiler_params=params(),
        name="conv_input",
    )(lax.axis_index("dp").reshape(1), got, *w_all)
    grad_all = lax.all_to_all(grad_sent, "rows", 0, 0).reshape(chans, total)

    qt, kt, key, value, att, top, inv, conv_terms = pl.pallas_call(
        lambda *refs: forward_kernel(width, *refs),
        out_shape=(
            jax.ShapeDtypeStruct((chans, total), BF16),
            jax.ShapeDtypeStruct((chans, total), BF16),
            jax.ShapeDtypeStruct((total, chans), BF16),
            jax.ShapeDtypeStruct((total, chans), BF16),
            jax.ShapeDtypeStruct((chans, total), F32),
            jax.ShapeDtypeStruct((1, total), F32),
            jax.ShapeDtypeStruct((1, total), F32),
            jax.ShapeDtypeStruct((slots, per * 32, chans), BF16),
        ),
        in_specs=[pl.BlockSpec(memory_space=pltpu.SMEM)] + whole(6),
        out_specs=tuple(whole(8)),
        scratch_shapes=[
            pltpu.VMEM((chans, total), BF16),
            pltpu.VMEM((9 * part, total + 2 * width), BF16),
            pltpu.VMEM((chans, total), BF16),
            pltpu.VMEM((chans // 128, 32 * part, 128), F32),
            pltpu.VMEM((total, cells), F32),
            pltpu.VMEM((total, cells), F32),
            pltpu.VMEM((total, cells), BF16),
        ],
        compiler_params=params(),
        name="forward",
    )(me.reshape(1), got, query_weight, key_weight, value_weight, out_weight, order_b)

    feature_grad, give, keep = pl.pallas_call(
        backward_kernel,
        out_shape=(
            jax.ShapeDtypeStruct((cells, chans), BF16),
            jax.ShapeDtypeStruct((pairs * groups * 8, 2 * chans), BF16),
            jax.ShapeDtypeStruct((pairs * groups * 8, 2 * chans), BF16),
        ),
        in_specs=[pl.BlockSpec(memory_space=pltpu.SMEM)] + whole(16),
        out_specs=tuple(whole(3)),
        scratch_shapes=[
            pltpu.VMEM((chans, total), BF16),
            pltpu.VMEM((1, total), F32),
            pltpu.VMEM((total, cells), BF16),
            pltpu.VMEM((cells, total), BF16),
            pltpu.VMEM((cells, total), BF16),
        ],
        compiler_params=params(),
        name="backward",
    )(
        jnp.stack([me, core]),
        x,
        grad_all,
        qt,
        kt,
        key,
        value,
        att,
        top,
        inv,
        query_weight,
        key_weight,
        value_weight,
        out_weight,
        order_b,
        back_b,
        by_core,
    )

    conv_sum = jnp.sum(lax.all_to_all(conv_terms, "dp", 0, 0).astype(F32), 0)
    conv_grad = conv_sum.reshape(per, 32, chans)[:, :27].reshape(per, 27 * chans)
    taken = lax.ppermute(give, "dp", [(d, d ^ 1) for d in range(slots)])
    chip = (keep.astype(F32) + taken.astype(F32)).astype(BF16)
    chip = chip.reshape(pairs * groups, 8, 2 * chans)
    same_core = [[d * groups + r for d in range(c, slots, 2) for r in range(groups)] for c in range(2)]
    chip = lax.all_to_all(chip, ("dp", "rows"), 0, 0, axis_index_groups=same_core)
    proj = jnp.sum(chip.astype(F32), 0).reshape(2, 4, 2, chans)[:, :per]
    proj_grads = proj.transpose(1, 0, 2, 3).reshape(per, 4 * chans)
    return feature_grad.reshape(features.shape), proj_grads, conv_grad


def solution(mesh):
    placed = (
        P("dp", None, "rows", None, None),
        P("dp", None, "rows", None, None),
        P("dp", None, "rows", None, None),
        P(),
        P(),
        P(),
        P(),
        P(("dp", "rows"), None, None),
    )
    return jax.shard_map(
        shards,
        mesh=mesh,
        in_specs=placed,
        out_specs=(
            P("dp", None, "rows", None, None),
            P(("dp", "rows"), None),
            P(("dp", "rows"), None),
        ),
        check_vma=False,
    )
```

```python
import jax
import jax.numpy as jnp
import numpy as np
from jax import lax
from jax.experimental import pallas as pl
from jax.experimental.pallas import tpu as pltpu
from jax.sharding import PartitionSpec as P

F32 = jnp.float32
BF16 = jnp.bfloat16
LOG2E = 1.4426950408889634


def nn(a, b):
    return lax.dot_general(a, b, (((1,), (0,)), ((), ())), preferred_element_type=F32)


def nt(a, b):
    return lax.dot_general(a, b, (((1,), (1,)), ((), ())), preferred_element_type=F32)


def whole(count):
    return [pl.BlockSpec(memory_space=pltpu.VMEM)] * count


def anywhere(count):
    return [pl.BlockSpec(memory_space=pl.ANY)] * count


def in_hbm(count):
    return [pl.BlockSpec(memory_space=pltpu.HBM)] * count


def params(mib):
    return pltpu.CompilerParams(vmem_limit_bytes=mib * 1024 * 1024)


def cost(macs, size):
    return pl.CostEstimate(flops=2 * macs, bytes_accessed=size, transcendentals=0)


def eye_of(n):
    rows = lax.broadcasted_iota(jnp.int32, (n, n), 0)
    cols = lax.broadcasted_iota(jnp.int32, (n, n), 1)
    return jnp.where(rows == cols, 1.0, 0.0).astype(BF16)


def pack_kernel(u_ref, past_ref, order_ref, conv_ref, out_ref, w_ref):
    chans = u_ref.shape[1]
    groups = out_ref.shape[0]
    part = chans // groups
    w_ref[...] = jnp.zeros(w_ref.shape, BF16)
    for k in range(w_ref.shape[0]):
        w_ref[k, 0:11, :] = conv_ref[k, 16:27, :]
    u_t = nt(eye_of(chans), u_ref[...]).astype(BF16)
    for r in range(groups):
        out_ref[r, 0:chans, :] = u_t
    for f in range(2):
        p_t = nt(order_ref[...], past_ref[f]).astype(BF16)
        for r in range(groups):
            at = chans + f * part
            out_ref[r, at : at + part, :] = p_t[r * part : (r + 1) * part]


def prepare_kernel(me_ref, wq_ref, wk_ref, wv_ref, wo_ref, order_ref, wqkv_t_ref, wkv_ref, pick_ref, wo_pick_ref, wo_order_ref):
    chans = wq_ref.shape[0]
    part = pick_ref.shape[0]
    eye = eye_of(chans)
    for n, ref in enumerate((wq_ref, wk_ref, wv_ref)):
        wqkv_t_ref[n * chans : (n + 1) * chans, :] = nt(eye, ref[...]).astype(BF16)
    wkv_ref[:, 0:chans] = wk_ref[...]
    wkv_ref[:, chans:] = wv_ref[...]
    pick = order_ref[pl.ds(pl.multiple_of(me_ref[0] * part, part), part), :]
    pick_ref[...] = pick
    wo_pick_ref[...] = nn(pick, nt(eye, wo_ref[...]).astype(BF16)).astype(BF16)
    wo_order_ref[...] = nt(wo_ref[...], order_ref[...]).astype(BF16)


def conv_input_kernel(width, me_ref, got_ref, w_mine_ref, w_other_ref, *refs):
    out_ref, wide_ref, w32_ref, wcat_ref, grad_ref, sems = refs[-6:]
    groups = got_ref.shape[0]
    cells = got_ref.shape[2]
    part, total = out_ref.shape[1:]
    near, padded, chans = w_mine_ref.shape
    slots = 2 * near
    per = part // slots
    z, y, core = lax.div(me_ref[0], 4), lax.rem(lax.div(me_ref[0], 2), 2), lax.rem(me_ref[0], 2)
    for apart, w_ref in enumerate((w_mine_ref, w_other_ref)):
        for n in range(near):
            at = lax.rem(z + 4 - n // 2, 4) * 4 + lax.rem(y + n % 2, 2) * 2 + lax.rem(core + apart, 2)
            at = pl.ds(pl.multiple_of(at * padded, padded), padded)
            for c in range(chans // 128):
                w32_ref[c, at, :] = w_ref[n, :, c * 128 : (c + 1) * 128].astype(F32)
    for c in range(chans // 128):
        lanes = slice(c * 128, (c + 1) * 128)
        for tap in range(9):
            for k in range(per):
                rows = w32_ref[c, pl.ds(k * 16 + 2 + tap, slots, stride=padded), :]
                at = tap * part + k * slots
                wcat_ref[at : at + slots, lanes] = rows.astype(BF16)
    wide_ref[:, 0:width] = jnp.zeros((9 * part, width), F32)
    wide_ref[:, width + total :] = jnp.zeros((9 * part, width), F32)
    for r in range(groups):
        wide_ref[:, width + r * cells : width + (r + 1) * cells] = nn(
            wcat_ref[...], got_ref[r, 0:chans, :]
        )
    lane = lax.broadcasted_iota(jnp.int32, (part, total), 1) % width
    sums = []
    for j in range(3):
        piece = None
        for i in range(3):
            tap = 3 * i + j
            at = (2 - i) * width
            term = wide_ref[tap * part : (tap + 1) * part, at : at + total]
            piece = term if piece is None else piece + term
        sums.append(piece)
    first = jnp.where(lane == width - 1, 0.0, pltpu.roll(sums[0], total - 1, 1))
    last = jnp.where(lane == 0, 0.0, pltpu.roll(sums[2], 1, 1))
    grad_ref[...] = (first + sums[1] + last).astype(BF16)
    copies = [pltpu.make_async_copy(grad_ref, out_ref.at[r], sems.at[r]) for r in range(groups)]
    for copy in copies:
        copy.start()
    for copy in copies:
        copy.wait()


def forward_kernel(
    width,
    place_ref,
    got_in,
    x0_in,
    x1_in,
    x2_in,
    x3_in,
    x4_in,
    x5_in,
    x6_in,
    x7_in,
    wqkv_t_ref,
    wkv_ref,
    pick_ref,
    wo_pick_ref,
    qt_out,
    kt_out,
    key_out,
    value_out,
    att_out,
    top_ref,
    inv_ref,
    give_ref,
    keep_ref,
    got_ref,
    x_ref,
    qt_ref,
    kt_ref,
    key_ref,
    value_ref,
    att_ref,
    in_sems,
    x_sems,
    out_sems,
    att_sems,
    vt_ref,
    side_ref,
    ut_ref,
    acc_ref,
    even_ref,
    odd_ref,
    raised_ref,
):
    groups, cells = got_ref.shape[0], got_ref.shape[2]
    chans = wkv_ref.shape[0]
    total = groups * cells
    part = chans // groups

    me = place_ref[0]
    fetches = []
    for n, ref in enumerate((x0_in, x1_in, x2_in, x3_in, x4_in, x5_in, x6_in, x7_in)):
        plane = lax.rem(lax.div(me, 2) + (0, 3, 1, 2)[n // 2], 4)
        at = plane * 2 + lax.rem(me + n % 2, 2)
        fetches.append(pltpu.make_async_copy(ref, x_ref.at[at], x_sems.at[n]))
    for r in range(groups):
        fetches.append(pltpu.make_async_copy(got_in.at[r], got_ref.at[r], in_sems.at[r]))
    for fetch in fetches:
        fetch.start()
    kept = [(qt_ref, qt_out), (kt_ref, kt_out), (key_ref, key_out), (value_ref, value_out)]
    keeps = [pltpu.make_async_copy(a, b, out_sems.at[n]) for n, (a, b) in enumerate(kept)]

    def keep_att(r):
        at = pl.ds(pl.multiple_of(r * cells, cells), cells)
        return pltpu.make_async_copy(att_ref.at[:, at], att_out.at[:, at], att_sems.at[r])

    scale = chans ** (-0.5)
    def project(r, carry):
        x = x_ref[r].astype(F32)
        recip = lax.rsqrt(jnp.mean(x * x, 1, keepdims=True) + 1e-06)
        normed = (x * recip).astype(BF16)
        at = pl.ds(pl.multiple_of(r * cells, cells), cells)
        qkv_t = nt(wqkv_t_ref[...], normed).astype(BF16)
        qt_ref[:, at] = qkv_t[0:chans]
        kt_ref[:, at] = qkv_t[chans : 2 * chans]
        vt_ref[:, at] = qkv_t[2 * chans :]
        kv = nn(normed, wkv_ref[...]).astype(BF16)
        key_ref[at, :] = kv[:, 0:chans]
        value_ref[at, :] = kv[:, chans:]
        return carry

    for fetch in fetches[:groups]:
        fetch.wait()
    lax.fori_loop(0, groups, project, 0, unroll=2)
    for fetch in fetches[groups:]:
        fetch.wait()
    for copy in keeps:
        copy.start()
    for r in range(groups):
        ut_ref[:, r * cells : (r + 1) * cells] = got_ref[r, 0:chans, :]

    for n in range(9):
        rows = slice(n * part, (n + 1) * part)
        side_ref[rows, 0:width] = jnp.zeros((part, width), BF16)
        side_ref[rows, width + total :] = jnp.zeros((part, width), BF16)

    lane = lax.broadcasted_iota(jnp.int32, (part, width), 1)

    def place(t, at, block):
        for n in range(0, cells, width):
            one = block[:, n : n + width]
            one32 = one.astype(F32)
            left = jnp.where(lane == 0, 0.0, pltpu.roll(one32, 1, 1))
            right = jnp.where(lane == width - 1, 0.0, pltpu.roll(one32, width - 1, 1))
            for j, moved in enumerate((left.astype(BF16), one, right.astype(BF16))):
                rows = slice((3 * t + j) * part, (3 * t + j + 1) * part)
                side_ref[rows, width + at + n : 2 * width + at + n] = moved

    for r in range(groups):
        for f in range(2):
            at = chans + f * part
            place(f, r * cells, got_ref[r, at : at + part, :])

    even_ref[...] = nn(key_ref[...], qt_ref[:, 0:cells])
    chunk = total // 4

    def attend(r, now_ref, later_ref):
        later = jnp.minimum(r + 1, groups - 1)
        at = pl.ds(pl.multiple_of(r * cells, cells), cells)
        later = pl.ds(pl.multiple_of(later * cells, cells), cells)
        top = jnp.max(now_ref[...], 0, keepdims=True)
        count = jnp.zeros((1, cells), F32)
        for b in range(4):
            rows = slice(b * chunk, (b + 1) * chunk)
            later_ref[rows] = nn(key_ref[rows], qt_ref[:, later])
            raised = jnp.exp2((now_ref[rows] - top) * (scale * LOG2E))
            count = count + jnp.sum(raised, 0, keepdims=True)
            raised_ref[rows] = raised.astype(BF16)
        inv = 1.0 / count
        att = nn(vt_ref[...], raised_ref[...]) * inv
        att_ref[:, at] = att
        keep_att(r).start()
        top_ref[:, at] = top
        inv_ref[:, at] = inv

    def attend_two(n, carry):
        attend(2 * n, even_ref, odd_ref)
        attend(2 * n + 1, odd_ref, even_ref)
        return carry

    lax.fori_loop(0, groups // 2, attend_two, 0)
    for r in range(groups):
        x_pick = nt(pick_ref[...], x_ref[r])
        att = att_ref[:, r * cells : (r + 1) * cells].astype(BF16)
        place(2, r * cells, (x_pick + nn(wo_pick_ref[...], att)).astype(BF16))

    lane_tiles = chans // 128
    acc_ref[:, 27 * part :, :] = jnp.zeros((lane_tiles, 5 * part, 128), F32)
    for i in range(3):
        block = nt(side_ref[:, i * width : i * width + total], ut_ref[...])
        for t in range(3):
            for j in range(3):
                tap, at = 9 * t + 3 * i + j, (3 * t + j) * part
                for c in range(lane_tiles):
                    acc_ref[c, tap * part : (tap + 1) * part, :] = block[
                        at : at + part, c * 128 : (c + 1) * 128
                    ]
    near = give_ref.shape[0]
    for core, to_ref in ((1 - place_ref[1], give_ref), (place_ref[1], keep_ref)):
        for n in range(near):
            first = (n % 4) * 4 + (n // 4) * 2 + core
            for k in range(part // (2 * near)):
                for c in range(lane_tiles):
                    rows = acc_ref[c, pl.ds(k * 2 * near + first, 32, stride=part), :]
                    to_ref[n, k * 32 : (k + 1) * 32, c * 128 : (c + 1) * 128] = rows.astype(BF16)
    for copy in keeps:
        copy.wait()
    for r in range(groups):
        keep_att(r).wait()


def backward_kernel(
    place_ref,
    x_ref,
    grad_in,
    qt_in,
    kt_in,
    key_in,
    value_in,
    att_in,
    rows_in,
    top_ref,
    inv_ref,
    wq_ref,
    wk_ref,
    wv_ref,
    wo_order_ref,
    back_ref,
    out_ref,
    give_ref,
    keep_ref,
    grad_ref,
    qt_ref,
    kt_ref,
    key_ref,
    value_ref,
    att_ref,
    rows_ref,
    sems,
    ga_ref,
    tot_ref,
    sq_ref,
    sk_ref,
    pb_ref,
    pq_ref,
    pk_ref,
):
    cells = x_ref.shape[0]
    chans, total = qt_ref.shape
    moves = [
        (key_in, key_ref),
        (qt_in, qt_ref),
        (grad_in, grad_ref),
        (att_in, att_ref),
        (value_in, value_ref),
        (kt_in, kt_ref),
        (rows_in, rows_ref),
    ]
    moves = [pltpu.make_async_copy(a, b, sems.at[n]) for n, (a, b) in enumerate(moves)]
    for copy in moves:
        copy.start()
    scale = chans ** (-0.5)
    mine = pl.ds(pl.multiple_of(place_ref[0] * cells, cells), cells)
    core = place_ref[1]
    chunk = total // 4
    chunks = [slice(b * chunk, (b + 1) * chunk) for b in range(4)]

    def probs_of(scores, top, inv):
        return jnp.exp2((scores - top) * (scale * LOG2E)) * inv

    for copy in moves[0:2]:
        copy.wait()
    key_mine = key_ref[mine, :]
    q_mine = qt_ref[:, mine]
    top_mine = top_ref[:, mine]
    inv_mine = inv_ref[:, mine]
    for at in chunks:
        pq_ref[at, :] = probs_of(nn(key_ref[at, :], q_mine), top_mine, inv_mine)
        pk_ref[:, at] = probs_of(nn(key_mine, qt_ref[:, at]), top_ref[:, at], inv_ref[:, at])
    for copy in moves[2:4]:
        copy.wait()
    for at in chunks:
        ga = nn(wo_order_ref[...], grad_ref[:, at]).astype(BF16)
        ga_ref[:, at] = ga
        tot_ref[:, at] = jnp.sum(att_ref[:, at] * ga.astype(F32), 0, keepdims=True)
    moves[4].wait()
    value_mine = value_ref[mine, :]
    ga_mine = ga_ref[:, mine]
    tot_mine = tot_ref[:, mine]
    for at in chunks:
        grad_probs = nn(value_ref[at, :], ga_mine)
        sq_ref[at, :] = (pq_ref[at, :] * (grad_probs - tot_mine) * scale).astype(BF16)
        probs = pk_ref[:, at]
        grad_probs = nn(value_mine, ga_ref[:, at])
        pb_ref[:, at] = probs.astype(BF16)
        sk_ref[:, at] = (probs * (grad_probs - tot_ref[:, at]) * scale).astype(BF16)

    moves[5].wait()
    gq = nn(kt_ref[...], sq_ref[...]).astype(BF16)
    gk = nt(qt_ref[...], sk_ref[...]).astype(BF16)
    gv = nt(ga_ref[...], pb_ref[...]).astype(BF16)
    x = nt(eye_of(chans), x_ref[...])
    recip = lax.rsqrt(jnp.mean(x * x, 0, keepdims=True) + 1e-06)
    normed = (x * recip).astype(BF16)
    grad_b = nn(back_ref[...], grad_ref[:, mine])
    grad_normed = nn(wq_ref[...], gq) + nn(wk_ref[...], gk) + nn(wv_ref[...], gv)
    inner = jnp.mean(grad_normed * x, 0, keepdims=True)
    out = grad_b + recip * grad_normed - x * (recip * recip * recip) * inner
    out_ref[...] = nt(eye_of(cells), out.astype(BF16)).astype(BF16)
    moves[6].wait()
    att = att_ref[:, mine].astype(BF16)
    gq_gv = jnp.concatenate([nt(eye_of(cells), gq), nt(eye_of(cells), gv)], 0).astype(BF16)
    gk_gb = jnp.concatenate(
        [nt(eye_of(cells), gk), nt(eye_of(cells), grad_b.astype(BF16))], 0
    ).astype(BF16)
    for half, to_ref in ((1 - core, give_ref), (core, keep_ref)):
        upper = nn(rows_ref[half, 0], normed).astype(BF16)
        lower = nn(rows_ref[half, 1], normed).astype(BF16)
        lower_att = nn(rows_ref[half, 1], att).astype(BF16)
        to_ref[:, 0:chans] = nn(jnp.concatenate([upper, lower], 1), gq_gv).astype(BF16)
        to_ref[:, chans:] = nn(jnp.concatenate([upper, lower_att], 1), gk_gb).astype(BF16)


def shards(
    features, past_frames, upstream, query_weight, key_weight, value_weight, out_weight, conv_weight
):
    slots, groups = lax.axis_size("dp"), lax.axis_size("rows")
    _, _, rows_here, width, chans = features.shape
    cells = rows_here * width
    total = cells * groups
    part = chans // groups
    per = part // slots
    me = lax.axis_index("rows")

    order = np.zeros((chans, chans), np.float32)
    for r in range(groups):
        for k in range(per):
            for d in range(slots):
                order[r * part + k * slots + d, d * per * groups + per * r + k] = 1.0
    order_b = jnp.asarray(order, BF16)
    back_b = jnp.asarray(order.T, BF16)

    pairs = slots // 2
    by_core = np.zeros((2, 2, pairs * groups * 8, chans), np.float32)
    for core in range(2):
        for pair in range(pairs):
            for r in range(groups):
                for k in range(per):
                    row = (pair * groups + r) * 8 + k
                    chan = (2 * pair + core) * per * groups + per * r + k
                    by_core[core, 0, row, chan] = 1.0
                    by_core[core, 1, row + 4, chan] = 1.0
    by_core = jnp.asarray(by_core, BF16)
    core = lax.rem(lax.axis_index("dp"), 2)

    x = features.reshape(cells, chans)
    u = upstream.reshape(cells, chans)
    past = past_frames.reshape(2, cells, chans)
    def across(block):
        return lax.ppermute(block, "rows", [(r, r ^ 1) for r in range(groups)])

    def along(block, step):
        return lax.ppermute(block, "rows", [(r, (r + 2 * step) % groups) for r in range(groups)])

    x_across = across(x)
    x_low, x_high = along(x, 1), along(x, -1)

    packed, w_local = pl.pallas_call(
        pack_kernel,
        out_shape=(
            jax.ShapeDtypeStruct((groups, chans + 2 * part, cells), BF16),
            jax.ShapeDtypeStruct((per, 16, chans), BF16),
        ),
        in_specs=whole(4),
        out_specs=tuple(whole(2)),
        compiler_params=params(56),
        name="pack",
    )(u, past, order_b, conv_weight)

    w_near = w_local.reshape(1, per * 16, chans)
    w_across = lax.ppermute(w_near, "dp", [(d, d ^ 2) for d in range(slots)])
    packed, w_across, x_across, x_low, x_high, place = lax.optimization_barrier(
        (packed, w_across, x_across, x_low, x_high, me.reshape(1))
    )
    x_low_across, x_high_across = along(x_across, 1), along(x_across, -1)
    x_far, x_far_across = along(x_low, 1), along(x_high_across, -1)
    x_all = (x, x_across, x_low, x_low_across, x_high, x_high_across, x_far, x_far_across)
    got = lax.all_to_all(packed, "rows", 0, 0)
    w_near = jnp.concatenate([w_near, w_across], 0)
    w_line = [w_near]
    for back in (1, 2, 3):
        w_line.append(lax.ppermute(w_near, "dp", [(d, (d + 4 * back) % slots) for d in range(slots)]))
    w_mine = jnp.concatenate(w_line, 0)
    w_other = lax.ppermute(w_mine, "dp", [(d, d ^ 1) for d in range(slots)])

    wqkv_t, wkv, pick, wo_pick, wo_order = pl.pallas_call(
        prepare_kernel,
        out_shape=(
            jax.ShapeDtypeStruct((3 * chans, chans), BF16),
            jax.ShapeDtypeStruct((chans, 2 * chans), BF16),
            jax.ShapeDtypeStruct((part, chans), BF16),
            jax.ShapeDtypeStruct((part, chans), BF16),
            jax.ShapeDtypeStruct((chans, chans), BF16),
        ),
        in_specs=[pl.BlockSpec(memory_space=pltpu.SMEM)] + whole(5),
        out_specs=tuple(whole(5)),
        compiler_params=params(56),
        name="prepare",
    )(place, query_weight, key_weight, value_weight, out_weight, order_b)

    grad_sent = pl.pallas_call(
        lambda *refs: conv_input_kernel(width, *refs),
        out_shape=jax.ShapeDtypeStruct((groups, part, total), BF16),
        in_specs=[pl.BlockSpec(memory_space=pltpu.SMEM)] + whole(3) + anywhere(5),
        out_specs=in_hbm(1)[0],
        scratch_shapes=[
            pltpu.VMEM((9 * part, total + 2 * width), F32),
            pltpu.VMEM((chans // 128, slots * per * 16, 128), F32),
            pltpu.VMEM((9 * part, chans), BF16),
            pltpu.VMEM((part, total), BF16),
            pltpu.SemaphoreType.DMA((groups,)),
        ],
        compiler_params=params(56),
        name="conv_input",
    )(lax.axis_index("dp").reshape(1), got, w_mine, w_other, wo_order, *x_all[3:4], *x_all[5:])
    grad_all = lax.all_to_all(grad_sent, "rows", 0, 0).reshape(chans, total)

    qt, kt, key, value, att, top, inv, conv_give, conv_keep = pl.pallas_call(
        lambda *refs: forward_kernel(width, *refs),
        out_shape=(
            jax.ShapeDtypeStruct((chans, total), BF16),
            jax.ShapeDtypeStruct((chans, total), BF16),
            jax.ShapeDtypeStruct((total, chans), BF16),
            jax.ShapeDtypeStruct((total, chans), BF16),
            jax.ShapeDtypeStruct((chans, total), F32),
            jax.ShapeDtypeStruct((1, total), F32),
            jax.ShapeDtypeStruct((1, total), F32),
            jax.ShapeDtypeStruct((slots // 2, per * 32, chans), BF16),
            jax.ShapeDtypeStruct((slots // 2, per * 32, chans), BF16),
        ),
        in_specs=[pl.BlockSpec(memory_space=pltpu.SMEM)] + anywhere(9) + whole(4),
        out_specs=tuple(anywhere(5) + whole(4)),
        scratch_shapes=[
            pltpu.VMEM(got.shape, BF16),
            pltpu.VMEM((groups, cells, chans), BF16),
            pltpu.VMEM((chans, total), BF16),
            pltpu.VMEM((chans, total), BF16),
            pltpu.VMEM((total, chans), BF16),
            pltpu.VMEM((total, chans), BF16),
            pltpu.VMEM((chans, total), F32),
            pltpu.SemaphoreType.DMA((groups,)),
            pltpu.SemaphoreType.DMA((groups,)),
            pltpu.SemaphoreType.DMA((4,)),
            pltpu.SemaphoreType.DMA((groups,)),
            pltpu.VMEM((chans, total), BF16),
            pltpu.VMEM((9 * part, total + 2 * width), BF16),
            pltpu.VMEM((chans, total), BF16),
            pltpu.VMEM((chans // 128, 32 * part, 128), F32),
            pltpu.VMEM((total, cells), F32),
            pltpu.VMEM((total, cells), F32),
            pltpu.VMEM((total, cells), BF16),
        ],
        compiler_params=params(56),
        name="forward",
    )(jnp.stack([me, core]), got, *x_all, wqkv_t, wkv, pick, wo_pick)
    conv_taken = lax.ppermute(conv_give, "dp", [(d, d ^ 1) for d in range(slots)])

    feature_grad, give, keep = pl.pallas_call(
        backward_kernel,
        out_shape=(
            jax.ShapeDtypeStruct((cells, chans), BF16),
            jax.ShapeDtypeStruct((pairs * groups * 8, 2 * chans), BF16),
            jax.ShapeDtypeStruct((pairs * groups * 8, 2 * chans), BF16),
        ),
        in_specs=[pl.BlockSpec(memory_space=pltpu.SMEM)] + whole(1) + anywhere(7) + whole(7),
        out_specs=tuple(whole(3)),
        scratch_shapes=[
            pltpu.VMEM((chans, total), BF16),
            pltpu.VMEM((chans, total), BF16),
            pltpu.VMEM((chans, total), BF16),
            pltpu.VMEM((total, chans), BF16),
            pltpu.VMEM((total, chans), BF16),
            pltpu.VMEM((chans, total), F32),
            pltpu.VMEM(by_core.shape, BF16),
            pltpu.SemaphoreType.DMA((7,)),
            pltpu.VMEM((chans, total), BF16),
            pltpu.VMEM((1, total), F32),
            pltpu.VMEM((total, cells), BF16),
            pltpu.VMEM((cells, total), BF16),
            pltpu.VMEM((cells, total), BF16),
            pltpu.VMEM((total, cells), F32),
            pltpu.VMEM((cells, total), F32),
        ],
        compiler_params=params(56),
        name="backward",
    )(
        jnp.stack([me, core]),
        x,
        grad_all,
        qt,
        kt,
        key,
        value,
        att,
        by_core,
        top,
        inv,
        query_weight,
        key_weight,
        value_weight,
        wo_order,
        back_b,
    )

    taken = lax.ppermute(give, "dp", [(d, d ^ 1) for d in range(slots)])
    chip = (keep.astype(F32) + taken.astype(F32)).astype(BF16)
    chip = chip.reshape(pairs * groups, 8, 2 * chans)
    same_core = [[d * groups + r for d in range(c, slots, 2) for r in range(groups)] for c in range(2)]
    conv_taken, chip = lax.optimization_barrier((conv_taken, chip))
    got_chip = lax.all_to_all(chip, ("dp", "rows"), 0, 0, axis_index_groups=same_core)
    me_dp = lax.axis_index("dp")
    z, y = lax.div(me_dp, 4), lax.rem(lax.div(me_dp, 2), 2)
    conv_line = conv_keep.astype(F32) + conv_taken.astype(F32)
    sent = lax.dynamic_slice_in_dim(conv_line, (1 - y) * 4, 4, 0).astype(BF16)
    taken = lax.ppermute(sent, "dp", [(d, d ^ 2) for d in range(slots)])
    conv_line = lax.dynamic_slice_in_dim(conv_line, y * 4, 4, 0) + taken.astype(F32)
    conv_sum = lax.dynamic_index_in_dim(conv_line, z, 0, keepdims=False)
    for on in (1, 2, 3):
        sent = lax.dynamic_index_in_dim(conv_line, lax.rem(z + on, 4), 0, keepdims=False).astype(BF16)
        taken = lax.ppermute(sent, "dp", [(d, (d + 4 * on) % slots) for d in range(slots)])
        conv_sum = conv_sum + taken.astype(F32)
    conv_grad = conv_sum.reshape(per, 32, chans)[:, :27].reshape(per, 27 * chans)
    proj = jnp.sum(got_chip.astype(F32), 0).reshape(2, 4, 2, chans)[:, :per]
    proj_grads = proj.transpose(1, 0, 2, 3).reshape(per, 4 * chans)
    return feature_grad.reshape(features.shape), proj_grads, conv_grad


def solution(mesh):
    placed = (
        P("dp", None, "rows", None, None),
        P("dp", None, "rows", None, None),
        P("dp", None, "rows", None, None),
        P(),
        P(),
        P(),
        P(),
        P(("dp", "rows"), None, None),
    )
    return jax.shard_map(
        shards,
        mesh=mesh,
        in_specs=placed,
        out_specs=(
            P("dp", None, "rows", None, None),
            P(("dp", "rows"), None),
            P(("dp", "rows"), None),
        ),
        check_vma=False,
    )
```

```python
import jax
import jax.numpy as jnp
import numpy as np
from jax import lax
from jax.experimental import pallas as pl
from jax.experimental.pallas import tpu as pltpu
from jax.sharding import PartitionSpec as P

F32 = jnp.float32
BF16 = jnp.bfloat16
LOG2E = 1.4426950408889634


def nn(a, b):
    return lax.dot_general(a, b, (((1,), (0,)), ((), ())), preferred_element_type=F32)


def nt(a, b):
    return lax.dot_general(a, b, (((1,), (1,)), ((), ())), preferred_element_type=F32)


def whole(count):
    return [pl.BlockSpec(memory_space=pltpu.VMEM)] * count


def anywhere(count):
    return [pl.BlockSpec(memory_space=pl.ANY)] * count


def in_hbm(count):
    return [pl.BlockSpec(memory_space=pltpu.HBM)] * count


def params(mib):
    return pltpu.CompilerParams(vmem_limit_bytes=mib * 1024 * 1024)


def cost(macs, size):
    return pl.CostEstimate(flops=2 * macs, bytes_accessed=size, transcendentals=0)


def eye_of(n):
    rows = lax.broadcasted_iota(jnp.int32, (n, n), 0)
    cols = lax.broadcasted_iota(jnp.int32, (n, n), 1)
    return jnp.where(rows == cols, 1.0, 0.0).astype(BF16)


def pack_kernel(u_ref, past_ref, order_ref, conv_ref, out_ref, w_ref):
    chans = u_ref.shape[1]
    groups = out_ref.shape[0]
    part = chans // groups
    w_ref[...] = jnp.zeros(w_ref.shape, BF16)
    for k in range(w_ref.shape[0]):
        w_ref[k, 0:11, :] = conv_ref[k, 16:27, :]
    u_t = nt(eye_of(chans), u_ref[...]).astype(BF16)
    for r in range(groups):
        out_ref[r, 0:chans, :] = u_t
    for f in range(2):
        p_t = nt(order_ref[...], past_ref[f]).astype(BF16)
        for r in range(groups):
            at = chans + f * part
            out_ref[r, at : at + part, :] = p_t[r * part : (r + 1) * part]


def prepare_kernel(me_ref, wq_ref, wk_ref, wv_ref, wo_ref, order_ref, wqkv_t_ref, wkv_ref, pick_ref, wo_pick_ref, wo_order_ref):
    chans = wq_ref.shape[0]
    part = pick_ref.shape[0]
    eye = eye_of(chans)
    for n, ref in enumerate((wq_ref, wk_ref, wv_ref)):
        wqkv_t_ref[n * chans : (n + 1) * chans, :] = nt(eye, ref[...]).astype(BF16)
    wkv_ref[:, 0:chans] = wk_ref[...]
    wkv_ref[:, chans:] = wv_ref[...]
    pick = order_ref[pl.ds(pl.multiple_of(me_ref[0] * part, part), part), :]
    pick_ref[...] = pick
    wo_pick_ref[...] = nn(pick, nt(eye, wo_ref[...]).astype(BF16)).astype(BF16)
    wo_order_ref[...] = nt(wo_ref[...], order_ref[...]).astype(BF16)


def conv_input_kernel(width, me_ref, got_ref, w_mine_ref, w_other_ref, *refs):
    out_ref, wide_ref, w32_ref, wcat_ref, grad_ref, sems = refs[-6:]
    groups = got_ref.shape[0]
    cells = got_ref.shape[2]
    part, total = out_ref.shape[1:]
    near, padded, chans = w_mine_ref.shape
    slots = 2 * near
    per = part // slots
    z, y, core = lax.div(me_ref[0], 4), lax.rem(lax.div(me_ref[0], 2), 2), lax.rem(me_ref[0], 2)
    for apart, w_ref in enumerate((w_mine_ref, w_other_ref)):
        for n in range(near):
            at = lax.rem(z + 4 - n // 2, 4) * 4 + lax.rem(y + n % 2, 2) * 2 + lax.rem(core + apart, 2)
            at = pl.ds(pl.multiple_of(at * padded, padded), padded)
            for c in range(chans // 128):
                w32_ref[c, at, :] = w_ref[n, :, c * 128 : (c + 1) * 128].astype(F32)
    for c in range(chans // 128):
        lanes = slice(c * 128, (c + 1) * 128)
        for tap in range(9):
            for k in range(per):
                rows = w32_ref[c, pl.ds(k * 16 + 2 + tap, slots, stride=padded), :]
                at = tap * part + k * slots
                wcat_ref[at : at + slots, lanes] = rows.astype(BF16)
    wide_ref[:, 0:width] = jnp.zeros((9 * part, width), F32)
    wide_ref[:, width + total :] = jnp.zeros((9 * part, width), F32)
    for r in range(groups):
        wide_ref[:, width + r * cells : width + (r + 1) * cells] = nn(
            wcat_ref[...], got_ref[r, 0:chans, :]
        )
    lane = lax.broadcasted_iota(jnp.int32, (part, total), 1) % width
    sums = []
    for j in range(3):
        piece = None
        for i in range(3):
            tap = 3 * i + j
            at = (2 - i) * width
            term = wide_ref[tap * part : (tap + 1) * part, at : at + total]
            piece = term if piece is None else piece + term
        sums.append(piece)
    first = jnp.where(lane == width - 1, 0.0, pltpu.roll(sums[0], total - 1, 1))
    last = jnp.where(lane == 0, 0.0, pltpu.roll(sums[2], 1, 1))
    grad_ref[...] = (first + sums[1] + last).astype(BF16)
    copies = [pltpu.make_async_copy(grad_ref, out_ref.at[r], sems.at[r]) for r in range(groups)]
    for copy in copies:
        copy.start()
    for copy in copies:
        copy.wait()


def forward_kernel(
    width,
    place_ref,
    got_in,
    x0_in,
    x1_in,
    x2_in,
    x3_in,
    x4_in,
    x5_in,
    x6_in,
    x7_in,
    wqkv_t_ref,
    wkv_ref,
    pick_ref,
    wo_pick_ref,
    qt_out,
    kt_out,
    key_out,
    value_out,
    att_out,
    top_ref,
    inv_ref,
    give_ref,
    keep_ref,
    got_ref,
    x_ref,
    qt_ref,
    kt_ref,
    key_ref,
    value_ref,
    att_ref,
    in_sems,
    x_sems,
    out_sems,
    att_sems,
    vt_ref,
    side_ref,
    ut_ref,
    acc_ref,
    even_ref,
    odd_ref,
    raised_ref,
):
    groups, cells = got_ref.shape[0], got_ref.shape[2]
    chans = wkv_ref.shape[0]
    total = groups * cells
    part = chans // groups

    me = place_ref[0]
    fetches = []
    for n, ref in enumerate((x0_in, x1_in, x2_in, x3_in, x4_in, x5_in, x6_in, x7_in)):
        plane = lax.rem(lax.div(me, 2) + (0, 3, 1, 2)[n // 2], 4)
        at = plane * 2 + lax.rem(me + n % 2, 2)
        fetches.append(pltpu.make_async_copy(ref, x_ref.at[at], x_sems.at[n]))
    for r in range(groups):
        fetches.append(pltpu.make_async_copy(got_in.at[r], got_ref.at[r], in_sems.at[r]))
    for fetch in fetches:
        fetch.start()
    kept = [(qt_ref, qt_out), (kt_ref, kt_out), (key_ref, key_out), (value_ref, value_out)]
    keeps = [pltpu.make_async_copy(a, b, out_sems.at[n]) for n, (a, b) in enumerate(kept)]

    def keep_att(r):
        at = pl.ds(pl.multiple_of(r * cells, cells), cells)
        return pltpu.make_async_copy(att_ref.at[:, at], att_out.at[:, at], att_sems.at[r])

    scale = chans ** (-0.5)
    def project(r, carry):
        x = x_ref[r].astype(F32)
        recip = lax.rsqrt(jnp.mean(x * x, 1, keepdims=True) + 1e-06)
        normed = (x * recip).astype(BF16)
        at = pl.ds(pl.multiple_of(r * cells, cells), cells)
        qkv_t = nt(wqkv_t_ref[...], normed).astype(BF16)
        qt_ref[:, at] = qkv_t[0:chans]
        kt_ref[:, at] = qkv_t[chans : 2 * chans]
        vt_ref[:, at] = qkv_t[2 * chans :]
        kv = nn(normed, wkv_ref[...]).astype(BF16)
        key_ref[at, :] = kv[:, 0:chans]
        value_ref[at, :] = kv[:, chans:]
        return carry

    for fetch in fetches[:groups]:
        fetch.wait()
    lax.fori_loop(0, groups, project, 0, unroll=2)
    for fetch in fetches[groups:]:
        fetch.wait()
    for copy in keeps:
        copy.start()
    for r in range(groups):
        ut_ref[:, r * cells : (r + 1) * cells] = got_ref[r, 0:chans, :]

    for n in range(9):
        rows = slice(n * part, (n + 1) * part)
        side_ref[rows, 0:width] = jnp.zeros((part, width), BF16)
        side_ref[rows, width + total :] = jnp.zeros((part, width), BF16)

    lane = lax.broadcasted_iota(jnp.int32, (part, width), 1)

    def place(t, at, block):
        for n in range(0, cells, width):
            one = block[:, n : n + width]
            one32 = one.astype(F32)
            left = jnp.where(lane == 0, 0.0, pltpu.roll(one32, 1, 1))
            right = jnp.where(lane == width - 1, 0.0, pltpu.roll(one32, width - 1, 1))
            for j, moved in enumerate((left.astype(BF16), one, right.astype(BF16))):
                rows = slice((3 * t + j) * part, (3 * t + j + 1) * part)
                side_ref[rows, width + at + n : 2 * width + at + n] = moved

    for r in range(groups):
        for f in range(2):
            at = chans + f * part
            place(f, r * cells, got_ref[r, at : at + part, :])

    even_ref[...] = nn(key_ref[...], qt_ref[:, 0:cells])
    chunk = total // 4

    def attend(r, now_ref, later_ref):
        later = jnp.minimum(r + 1, groups - 1)
        at = pl.ds(pl.multiple_of(r * cells, cells), cells)
        later = pl.ds(pl.multiple_of(later * cells, cells), cells)
        top = jnp.max(now_ref[...], 0, keepdims=True)
        count = jnp.zeros((1, cells), F32)
        for b in range(4):
            rows = slice(b * chunk, (b + 1) * chunk)
            later_ref[rows] = nn(key_ref[rows], qt_ref[:, later])
            raised = jnp.exp2((now_ref[rows] - top) * (scale * LOG2E))
            count = count + jnp.sum(raised, 0, keepdims=True)
            raised_ref[rows] = raised.astype(BF16)
        inv = 1.0 / count
        att = nn(vt_ref[...], raised_ref[...]) * inv
        att_ref[:, at] = att
        keep_att(r).start()
        top_ref[:, at] = top
        inv_ref[:, at] = inv

    def attend_two(n, carry):
        attend(2 * n, even_ref, odd_ref)
        attend(2 * n + 1, odd_ref, even_ref)
        return carry

    lax.fori_loop(0, groups // 2, attend_two, 0)
    for r in range(groups):
        x_pick = nt(pick_ref[...], x_ref[r])
        att = att_ref[:, r * cells : (r + 1) * cells].astype(BF16)
        place(2, r * cells, (x_pick + nn(wo_pick_ref[...], att)).astype(BF16))

    lane_tiles = chans // 128
    acc_ref[:, 27 * part :, :] = jnp.zeros((lane_tiles, 5 * part, 128), F32)
    for i in range(3):
        block = nt(side_ref[:, i * width : i * width + total], ut_ref[...])
        for t in range(3):
            for j in range(3):
                tap, at = 9 * t + 3 * i + j, (3 * t + j) * part
                for c in range(lane_tiles):
                    acc_ref[c, tap * part : (tap + 1) * part, :] = block[
                        at : at + part, c * 128 : (c + 1) * 128
                    ]
    near = give_ref.shape[0]
    for core, to_ref in ((1 - place_ref[1], give_ref), (place_ref[1], keep_ref)):
        for n in range(near):
            first = (n % 4) * 4 + (n // 4) * 2 + core
            for k in range(part // (2 * near)):
                for c in range(lane_tiles):
                    rows = acc_ref[c, pl.ds(k * 2 * near + first, 32, stride=part), :]
                    to_ref[n, k * 32 : (k + 1) * 32, c * 128 : (c + 1) * 128] = rows.astype(BF16)
    for copy in keeps:
        copy.wait()
    for r in range(groups):
        keep_att(r).wait()


def features_kernel(x_ref, gq_ref, gk_ref, gv_ref, gb_ref, wq_ref, wk_ref, wv_ref, out_ref):
    cells, chans = x_ref.shape
    x = nt(eye_of(chans), x_ref[...])
    recip = lax.rsqrt(jnp.mean(x * x, 0, keepdims=True) + 1e-06)
    grad_normed = (
        nn(wq_ref[...], gq_ref[...]) + nn(wk_ref[...], gk_ref[...]) + nn(wv_ref[...], gv_ref[...])
    )
    inner = jnp.mean(grad_normed * x, 0, keepdims=True)
    out = gb_ref[...].astype(F32) + recip * grad_normed - x * (recip * recip * recip) * inner
    out_ref[...] = nt(eye_of(cells), out.astype(BF16)).astype(BF16)


def backward_kernel(
    place_ref,
    x_ref,
    grad_in,
    qt_in,
    kt_in,
    key_in,
    value_in,
    att_in,
    rows_in,
    top_ref,
    inv_ref,
    wo_order_ref,
    back_ref,
    gq_ref,
    gk_ref,
    gv_ref,
    gb_ref,
    give_ref,
    keep_ref,
    grad_ref,
    qt_ref,
    kt_ref,
    key_ref,
    value_ref,
    att_ref,
    rows_ref,
    sems,
    ga_ref,
    tot_ref,
    sq_ref,
    sk_ref,
    pb_ref,
    pq_ref,
    pk_ref,
):
    cells = x_ref.shape[0]
    chans, total = qt_ref.shape
    moves = [
        (key_in, key_ref),
        (qt_in, qt_ref),
        (grad_in, grad_ref),
        (att_in, att_ref),
        (value_in, value_ref),
        (kt_in, kt_ref),
        (rows_in, rows_ref),
    ]
    moves = [pltpu.make_async_copy(a, b, sems.at[n]) for n, (a, b) in enumerate(moves)]
    for copy in moves:
        copy.start()
    scale = chans ** (-0.5)
    mine = pl.ds(pl.multiple_of(place_ref[0] * cells, cells), cells)
    core = place_ref[1]
    chunk = total // 4
    chunks = [slice(b * chunk, (b + 1) * chunk) for b in range(4)]

    def probs_of(scores, top, inv):
        return jnp.exp2((scores - top) * (scale * LOG2E)) * inv

    for copy in moves[0:2]:
        copy.wait()
    key_mine = key_ref[mine, :]
    q_mine = qt_ref[:, mine]
    top_mine = top_ref[:, mine]
    inv_mine = inv_ref[:, mine]
    for at in chunks:
        pq_ref[at, :] = probs_of(nn(key_ref[at, :], q_mine), top_mine, inv_mine)
        pk_ref[:, at] = probs_of(nn(key_mine, qt_ref[:, at]), top_ref[:, at], inv_ref[:, at])
    for copy in moves[2:4]:
        copy.wait()
    for at in chunks:
        ga = nn(wo_order_ref[...], grad_ref[:, at]).astype(BF16)
        ga_ref[:, at] = ga
        tot_ref[:, at] = jnp.sum(att_ref[:, at] * ga.astype(F32), 0, keepdims=True)
    moves[4].wait()
    value_mine = value_ref[mine, :]
    ga_mine = ga_ref[:, mine]
    tot_mine = tot_ref[:, mine]
    for at in chunks:
        grad_probs = nn(value_ref[at, :], ga_mine)
        sq_ref[at, :] = (pq_ref[at, :] * (grad_probs - tot_mine) * scale).astype(BF16)
        probs = pk_ref[:, at]
        grad_probs = nn(value_mine, ga_ref[:, at])
        pb_ref[:, at] = probs.astype(BF16)
        sk_ref[:, at] = (probs * (grad_probs - tot_ref[:, at]) * scale).astype(BF16)

    moves[5].wait()
    gq = nn(kt_ref[...], sq_ref[...]).astype(BF16)
    gk = nt(qt_ref[...], sk_ref[...]).astype(BF16)
    gv = nt(ga_ref[...], pb_ref[...]).astype(BF16)
    gq_ref[...] = gq
    gk_ref[...] = gk
    gv_ref[...] = gv
    x = nt(eye_of(chans), x_ref[...])
    recip = lax.rsqrt(jnp.mean(x * x, 0, keepdims=True) + 1e-06)
    normed = (x * recip).astype(BF16)
    grad_b = nn(back_ref[...], grad_ref[:, mine])
    gb_ref[...] = grad_b.astype(BF16)
    moves[6].wait()
    att = att_ref[:, mine].astype(BF16)
    gq_gv = jnp.concatenate([nt(eye_of(cells), gq), nt(eye_of(cells), gv)], 0).astype(BF16)
    gk_gb = jnp.concatenate(
        [nt(eye_of(cells), gk), nt(eye_of(cells), grad_b.astype(BF16))], 0
    ).astype(BF16)
    for half, to_ref in ((1 - core, give_ref), (core, keep_ref)):
        upper = nn(rows_ref[half, 0], normed).astype(BF16)
        lower = nn(rows_ref[half, 1], normed).astype(BF16)
        lower_att = nn(rows_ref[half, 1], att).astype(BF16)
        to_ref[:, 0:chans] = nn(jnp.concatenate([upper, lower], 1), gq_gv).astype(BF16)
        to_ref[:, chans:] = nn(jnp.concatenate([upper, lower_att], 1), gk_gb).astype(BF16)


def shards(
    features, past_frames, upstream, query_weight, key_weight, value_weight, out_weight, conv_weight
):
    slots, groups = lax.axis_size("dp"), lax.axis_size("rows")
    _, _, rows_here, width, chans = features.shape
    cells = rows_here * width
    total = cells * groups
    part = chans // groups
    per = part // slots
    me = lax.axis_index("rows")

    order = np.zeros((chans, chans), np.float32)
    for r in range(groups):
        for k in range(per):
            for d in range(slots):
                order[r * part + k * slots + d, d * per * groups + per * r + k] = 1.0
    order_b = jnp.asarray(order, BF16)
    back_b = jnp.asarray(order.T, BF16)

    pairs = slots // 2
    by_core = np.zeros((2, 2, pairs * groups * 8, chans), np.float32)
    for core in range(2):
        for pair in range(pairs):
            for r in range(groups):
                for k in range(per):
                    row = (pair * groups + r) * 8 + k
                    chan = (2 * pair + core) * per * groups + per * r + k
                    by_core[core, 0, row, chan] = 1.0
                    by_core[core, 1, row + 4, chan] = 1.0
    by_core = jnp.asarray(by_core, BF16)
    core = lax.rem(lax.axis_index("dp"), 2)

    x = features.reshape(cells, chans)
    u = upstream.reshape(cells, chans)
    past = past_frames.reshape(2, cells, chans)
    def across(block):
        return lax.ppermute(block, "rows", [(r, r ^ 1) for r in range(groups)])

    def along(block, step):
        return lax.ppermute(block, "rows", [(r, (r + 2 * step) % groups) for r in range(groups)])

    x_across = across(x)
    x_low, x_high = along(x, 1), along(x, -1)

    packed, w_local = pl.pallas_call(
        pack_kernel,
        out_shape=(
            jax.ShapeDtypeStruct((groups, chans + 2 * part, cells), BF16),
            jax.ShapeDtypeStruct((per, 16, chans), BF16),
        ),
        in_specs=whole(4),
        out_specs=tuple(whole(2)),
        compiler_params=params(56),
        name="pack",
    )(u, past, order_b, conv_weight)

    w_near = w_local.reshape(1, per * 16, chans)
    w_across = lax.ppermute(w_near, "dp", [(d, d ^ 2) for d in range(slots)])
    packed, w_across, x_across, x_low, x_high, place = lax.optimization_barrier(
        (packed, w_across, x_across, x_low, x_high, me.reshape(1))
    )
    x_low_across, x_high_across = along(x_across, 1), along(x_across, -1)
    x_far, x_far_across = along(x_low, 1), along(x_high_across, -1)
    x_all = (x, x_across, x_low, x_low_across, x_high, x_high_across, x_far, x_far_across)
    got = lax.all_to_all(packed, "rows", 0, 0)
    wqkv_t, wkv, pick, wo_pick, wo_order = pl.pallas_call(
        prepare_kernel,
        out_shape=(
            jax.ShapeDtypeStruct((3 * chans, chans), BF16),
            jax.ShapeDtypeStruct((chans, 2 * chans), BF16),
            jax.ShapeDtypeStruct((part, chans), BF16),
            jax.ShapeDtypeStruct((part, chans), BF16),
            jax.ShapeDtypeStruct((chans, chans), BF16),
        ),
        in_specs=[pl.BlockSpec(memory_space=pltpu.SMEM)] + whole(5),
        out_specs=tuple(whole(5)),
        compiler_params=params(56),
        name="prepare",
    )(place, query_weight, key_weight, value_weight, out_weight, order_b)

    w_across, wo_order = lax.optimization_barrier((w_across, wo_order))
    w_near = jnp.concatenate([w_near, w_across], 0)
    w_line = [w_near]
    for back in (1, 2, 3):
        w_line.append(lax.ppermute(w_near, "dp", [(d, (d + 4 * back) % slots) for d in range(slots)]))
    w_mine = jnp.concatenate(w_line, 0)
    w_other = lax.ppermute(w_mine, "dp", [(d, d ^ 1) for d in range(slots)])

    grad_sent = pl.pallas_call(
        lambda *refs: conv_input_kernel(width, *refs),
        out_shape=jax.ShapeDtypeStruct((groups, part, total), BF16),
        in_specs=[pl.BlockSpec(memory_space=pltpu.SMEM)] + whole(3),
        out_specs=in_hbm(1)[0],
        scratch_shapes=[
            pltpu.VMEM((9 * part, total + 2 * width), F32),
            pltpu.VMEM((chans // 128, slots * per * 16, 128), F32),
            pltpu.VMEM((9 * part, chans), BF16),
            pltpu.VMEM((part, total), BF16),
            pltpu.SemaphoreType.DMA((groups,)),
        ],
        compiler_params=params(56),
        name="conv_input",
    )(lax.axis_index("dp").reshape(1), got, w_mine, w_other)
    grad_sent, x_all = lax.optimization_barrier((grad_sent, x_all))
    grad_all = lax.all_to_all(grad_sent, "rows", 0, 0).reshape(chans, total)

    qt, kt, key, value, att, top, inv, conv_give, conv_keep = pl.pallas_call(
        lambda *refs: forward_kernel(width, *refs),
        out_shape=(
            jax.ShapeDtypeStruct((chans, total), BF16),
            jax.ShapeDtypeStruct((chans, total), BF16),
            jax.ShapeDtypeStruct((total, chans), BF16),
            jax.ShapeDtypeStruct((total, chans), BF16),
            jax.ShapeDtypeStruct((chans, total), F32),
            jax.ShapeDtypeStruct((1, total), F32),
            jax.ShapeDtypeStruct((1, total), F32),
            jax.ShapeDtypeStruct((slots // 2, per * 32, chans), BF16),
            jax.ShapeDtypeStruct((slots // 2, per * 32, chans), BF16),
        ),
        in_specs=[pl.BlockSpec(memory_space=pltpu.SMEM)] + anywhere(9) + whole(4),
        out_specs=tuple(anywhere(5) + whole(4)),
        scratch_shapes=[
            pltpu.VMEM(got.shape, BF16),
            pltpu.VMEM((groups, cells, chans), BF16),
            pltpu.VMEM((chans, total), BF16),
            pltpu.VMEM((chans, total), BF16),
            pltpu.VMEM((total, chans), BF16),
            pltpu.VMEM((total, chans), BF16),
            pltpu.VMEM((chans, total), F32),
            pltpu.SemaphoreType.DMA((groups,)),
            pltpu.SemaphoreType.DMA((groups,)),
            pltpu.SemaphoreType.DMA((4,)),
            pltpu.SemaphoreType.DMA((groups,)),
            pltpu.VMEM((chans, total), BF16),
            pltpu.VMEM((9 * part, total + 2 * width), BF16),
            pltpu.VMEM((chans, total), BF16),
            pltpu.VMEM((chans // 128, 32 * part, 128), F32),
            pltpu.VMEM((total, cells), F32),
            pltpu.VMEM((total, cells), F32),
            pltpu.VMEM((total, cells), BF16),
        ],
        compiler_params=params(56),
        name="forward",
    )(jnp.stack([me, core]), got, *x_all, wqkv_t, wkv, pick, wo_pick)
    conv_taken = lax.ppermute(conv_give, "dp", [(d, d ^ 1) for d in range(slots)])

    gq, gk, gv, gb, give, keep = pl.pallas_call(
        backward_kernel,
        out_shape=(
            jax.ShapeDtypeStruct((chans, cells), BF16),
            jax.ShapeDtypeStruct((chans, cells), BF16),
            jax.ShapeDtypeStruct((chans, cells), BF16),
            jax.ShapeDtypeStruct((chans, cells), BF16),
            jax.ShapeDtypeStruct((pairs * groups * 8, 2 * chans), BF16),
            jax.ShapeDtypeStruct((pairs * groups * 8, 2 * chans), BF16),
        ),
        in_specs=[pl.BlockSpec(memory_space=pltpu.SMEM)] + whole(1) + anywhere(7) + whole(4),
        out_specs=tuple(whole(6)),
        scratch_shapes=[
            pltpu.VMEM((chans, total), BF16),
            pltpu.VMEM((chans, total), BF16),
            pltpu.VMEM((chans, total), BF16),
            pltpu.VMEM((total, chans), BF16),
            pltpu.VMEM((total, chans), BF16),
            pltpu.VMEM((chans, total), F32),
            pltpu.VMEM(by_core.shape, BF16),
            pltpu.SemaphoreType.DMA((7,)),
            pltpu.VMEM((chans, total), BF16),
            pltpu.VMEM((1, total), F32),
            pltpu.VMEM((total, cells), BF16),
            pltpu.VMEM((cells, total), BF16),
            pltpu.VMEM((cells, total), BF16),
            pltpu.VMEM((total, cells), F32),
            pltpu.VMEM((cells, total), F32),
        ],
        compiler_params=params(56),
        name="backward",
    )(
        jnp.stack([me, core]),
        x,
        grad_all,
        qt,
        kt,
        key,
        value,
        att,
        by_core,
        top,
        inv,
        wo_order,
        back_b,
    )

    taken = lax.ppermute(give, "dp", [(d, d ^ 1) for d in range(slots)])
    chip = (keep.astype(F32) + taken.astype(F32)).astype(BF16)
    chip = chip.reshape(pairs * groups, 8, 2 * chans)
    same_core = [[d * groups + r for d in range(c, slots, 2) for r in range(groups)] for c in range(2)]
    conv_taken, chip, gb = lax.optimization_barrier((conv_taken, chip, gb))
    got_chip = lax.all_to_all(chip, ("dp", "rows"), 0, 0, axis_index_groups=same_core)
    feature_grad = pl.pallas_call(
        features_kernel,
        out_shape=jax.ShapeDtypeStruct((cells, chans), BF16),
        in_specs=whole(8),
        out_specs=pl.BlockSpec(memory_space=pltpu.VMEM),
        compiler_params=params(56),
        name="features",
    )(x, gq, gk, gv, gb, query_weight, key_weight, value_weight)
    me_dp = lax.axis_index("dp")
    z, y = lax.div(me_dp, 4), lax.rem(lax.div(me_dp, 2), 2)
    conv_line = conv_keep.astype(F32) + conv_taken.astype(F32)
    sent = lax.dynamic_slice_in_dim(conv_line, (1 - y) * 4, 4, 0).astype(BF16)
    taken = lax.ppermute(sent, "dp", [(d, d ^ 2) for d in range(slots)])
    conv_line = lax.dynamic_slice_in_dim(conv_line, y * 4, 4, 0) + taken.astype(F32)
    conv_sum = lax.dynamic_index_in_dim(conv_line, z, 0, keepdims=False)
    for on in (1, 2, 3):
        sent = lax.dynamic_index_in_dim(conv_line, lax.rem(z + on, 4), 0, keepdims=False).astype(BF16)
        taken = lax.ppermute(sent, "dp", [(d, (d + 4 * on) % slots) for d in range(slots)])
        conv_sum = conv_sum + taken.astype(F32)
    conv_grad = conv_sum.reshape(per, 32, chans)[:, :27].reshape(per, 27 * chans)
    proj = jnp.sum(got_chip.astype(F32), 0).reshape(2, 4, 2, chans)[:, :per]
    proj_grads = proj.transpose(1, 0, 2, 3).reshape(per, 4 * chans)
    return feature_grad.reshape(features.shape), proj_grads, conv_grad


def solution(mesh):
    placed = (
        P("dp", None, "rows", None, None),
        P("dp", None, "rows", None, None),
        P("dp", None, "rows", None, None),
        P(),
        P(),
        P(),
        P(),
        P(("dp", "rows"), None, None),
    )
    return jax.shard_map(
        shards,
        mesh=mesh,
        in_specs=placed,
        out_specs=(
            P("dp", None, "rows", None, None),
            P(("dp", "rows"), None),
            P(("dp", "rows"), None),
        ),
        check_vma=False,
    )
```

```python
import jax
import jax.numpy as jnp
import numpy as np
from jax import lax
from jax.experimental import pallas as pl
from jax.experimental.pallas import tpu as pltpu
from jax.sharding import PartitionSpec as P

F32 = jnp.float32
BF16 = jnp.bfloat16
LOG2E = 1.4426950408889634


def nn(a, b):
    return lax.dot_general(a, b, (((1,), (0,)), ((), ())), preferred_element_type=F32)


def nt(a, b):
    return lax.dot_general(a, b, (((1,), (1,)), ((), ())), preferred_element_type=F32)


def whole(count):
    return [pl.BlockSpec(memory_space=pltpu.VMEM)] * count


def anywhere(count):
    return [pl.BlockSpec(memory_space=pl.ANY)] * count


def in_hbm(count):
    return [pl.BlockSpec(memory_space=pltpu.HBM)] * count


def params(mib):
    return pltpu.CompilerParams(vmem_limit_bytes=mib * 1024 * 1024)


def cost(macs, size):
    return pl.CostEstimate(flops=2 * macs, bytes_accessed=size, transcendentals=0)


def eye_of(n):
    rows = lax.broadcasted_iota(jnp.int32, (n, n), 0)
    cols = lax.broadcasted_iota(jnp.int32, (n, n), 1)
    return jnp.where(rows == cols, 1.0, 0.0).astype(BF16)


def pack_kernel(u_ref, past_ref, order_ref, conv_ref, out_ref, w_ref):
    chans = u_ref.shape[1]
    groups = out_ref.shape[0]
    part = chans // groups
    w_ref[...] = jnp.zeros(w_ref.shape, BF16)
    for k in range(w_ref.shape[0]):
        w_ref[k, 0:11, :] = conv_ref[k, 16:27, :]
    u_t = nt(eye_of(chans), u_ref[...]).astype(BF16)
    for r in range(groups):
        out_ref[r, 0:chans, :] = u_t
    for f in range(2):
        p_t = nt(order_ref[...], past_ref[f]).astype(BF16)
        for r in range(groups):
            at = chans + f * part
            out_ref[r, at : at + part, :] = p_t[r * part : (r + 1) * part]


def prepare_kernel(me_ref, wq_ref, wk_ref, wv_ref, wo_ref, order_ref, wqkv_t_ref, wkv_ref, pick_ref, wo_pick_ref, wo_order_ref):
    chans = wq_ref.shape[0]
    part = pick_ref.shape[0]
    eye = eye_of(chans)
    for n, ref in enumerate((wq_ref, wk_ref, wv_ref)):
        wqkv_t_ref[n * chans : (n + 1) * chans, :] = nt(eye, ref[...]).astype(BF16)
    wkv_ref[:, 0:chans] = wk_ref[...]
    wkv_ref[:, chans:] = wv_ref[...]
    pick = order_ref[pl.ds(pl.multiple_of(me_ref[0] * part, part), part), :]
    pick_ref[...] = pick
    wo_pick_ref[...] = nn(pick, nt(eye, wo_ref[...]).astype(BF16)).astype(BF16)
    wo_order_ref[...] = nt(wo_ref[...], order_ref[...]).astype(BF16)


def conv_input_kernel(width, me_ref, got_ref, w_mine_ref, w_other_ref, *refs):
    out_ref, wide_ref, w32_ref, wcat_ref, grad_ref, sems = refs[-6:]
    groups = got_ref.shape[0]
    cells = got_ref.shape[2]
    part, total = out_ref.shape[1:]
    near, padded, chans = w_mine_ref.shape
    slots = 2 * near
    per = part // slots
    z, y, core = lax.div(me_ref[0], 4), lax.rem(lax.div(me_ref[0], 2), 2), lax.rem(me_ref[0], 2)
    for apart, w_ref in enumerate((w_mine_ref, w_other_ref)):
        for n in range(near):
            at = lax.rem(z + 4 - n // 2, 4) * 4 + lax.rem(y + n % 2, 2) * 2 + lax.rem(core + apart, 2)
            at = pl.ds(pl.multiple_of(at * padded, padded), padded)
            for c in range(chans // 128):
                w32_ref[c, at, :] = w_ref[n, :, c * 128 : (c + 1) * 128].astype(F32)
    for c in range(chans // 128):
        lanes = slice(c * 128, (c + 1) * 128)
        for tap in range(9):
            for k in range(per):
                rows = w32_ref[c, pl.ds(k * 16 + 2 + tap, slots, stride=padded), :]
                at = tap * part + k * slots
                wcat_ref[at : at + slots, lanes] = rows.astype(BF16)
    wide_ref[:, 0:width] = jnp.zeros((9 * part, width), F32)
    wide_ref[:, width + total :] = jnp.zeros((9 * part, width), F32)
    for r in range(groups):
        wide_ref[:, width + r * cells : width + (r + 1) * cells] = nn(
            wcat_ref[...], got_ref[r, 0:chans, :]
        )
    lane = lax.broadcasted_iota(jnp.int32, (part, total), 1) % width
    sums = []
    for j in range(3):
        piece = None
        for i in range(3):
            tap = 3 * i + j
            at = (2 - i) * width
            term = wide_ref[tap * part : (tap + 1) * part, at : at + total]
            piece = term if piece is None else piece + term
        sums.append(piece)
    first = jnp.where(lane == width - 1, 0.0, pltpu.roll(sums[0], total - 1, 1))
    last = jnp.where(lane == 0, 0.0, pltpu.roll(sums[2], 1, 1))
    grad_ref[...] = (first + sums[1] + last).astype(BF16)
    copies = [pltpu.make_async_copy(grad_ref, out_ref.at[r], sems.at[r]) for r in range(groups)]
    for copy in copies:
        copy.start()
    for copy in copies:
        copy.wait()


def forward_kernel(
    width,
    place_ref,
    got_in,
    x0_in,
    x1_in,
    x2_in,
    x3_in,
    x4_in,
    x5_in,
    x6_in,
    x7_in,
    wqkv_t_ref,
    wkv_ref,
    pick_ref,
    wo_pick_ref,
    qt_out,
    kt_out,
    key_out,
    value_out,
    att_out,
    top_ref,
    inv_ref,
    give_ref,
    keep_ref,
    got_ref,
    x_ref,
    qt_ref,
    kt_ref,
    key_ref,
    value_ref,
    att_ref,
    in_sems,
    x_sems,
    out_sems,
    att_sems,
    vt_ref,
    side_ref,
    ut_ref,
    acc_ref,
    even_ref,
    odd_ref,
    raised_ref,
):
    groups, cells = got_ref.shape[0], got_ref.shape[2]
    chans = wkv_ref.shape[0]
    total = groups * cells
    part = chans // groups

    me = place_ref[0]
    fetches = []
    for n, ref in enumerate((x0_in, x1_in, x2_in, x3_in, x4_in, x5_in, x6_in, x7_in)):
        plane = lax.rem(lax.div(me, 2) + (0, 3, 1, 2)[n // 2], 4)
        at = plane * 2 + lax.rem(me + n % 2, 2)
        fetches.append(pltpu.make_async_copy(ref, x_ref.at[at], x_sems.at[n]))
    for r in range(groups):
        fetches.append(pltpu.make_async_copy(got_in.at[r], got_ref.at[r], in_sems.at[r]))
    for fetch in fetches:
        fetch.start()
    kept = [(qt_ref, qt_out), (kt_ref, kt_out), (key_ref, key_out), (value_ref, value_out)]
    keeps = [pltpu.make_async_copy(a, b, out_sems.at[n]) for n, (a, b) in enumerate(kept)]

    def keep_att(r):
        at = pl.ds(pl.multiple_of(r * cells, cells), cells)
        return pltpu.make_async_copy(att_ref.at[:, at], att_out.at[:, at], att_sems.at[r])

    scale = chans ** (-0.5)
    def project(r, carry):
        x = x_ref[r].astype(F32)
        recip = lax.rsqrt(jnp.mean(x * x, 1, keepdims=True) + 1e-06)
        normed = (x * recip).astype(BF16)
        at = pl.ds(pl.multiple_of(r * cells, cells), cells)
        qkv_t = nt(wqkv_t_ref[...], normed).astype(BF16)
        qt_ref[:, at] = qkv_t[0:chans]
        kt_ref[:, at] = qkv_t[chans : 2 * chans]
        vt_ref[:, at] = qkv_t[2 * chans :]
        kv = nn(normed, wkv_ref[...]).astype(BF16)
        key_ref[at, :] = kv[:, 0:chans]
        value_ref[at, :] = kv[:, chans:]
        return carry

    for fetch in fetches[:groups]:
        fetch.wait()
    lax.fori_loop(0, groups, project, 0, unroll=2)
    for fetch in fetches[groups:]:
        fetch.wait()
    for copy in keeps:
        copy.start()
    for r in range(groups):
        ut_ref[:, r * cells : (r + 1) * cells] = got_ref[r, 0:chans, :]

    for n in range(9):
        rows = slice(n * part, (n + 1) * part)
        side_ref[rows, 0:width] = jnp.zeros((part, width), BF16)
        side_ref[rows, width + total :] = jnp.zeros((part, width), BF16)

    lane = lax.broadcasted_iota(jnp.int32, (part, width), 1)

    def place(t, at, block):
        for n in range(0, cells, width):
            one = block[:, n : n + width]
            one32 = one.astype(F32)
            left = jnp.where(lane == 0, 0.0, pltpu.roll(one32, 1, 1))
            right = jnp.where(lane == width - 1, 0.0, pltpu.roll(one32, width - 1, 1))
            for j, moved in enumerate((left.astype(BF16), one, right.astype(BF16))):
                rows = slice((3 * t + j) * part, (3 * t + j + 1) * part)
                side_ref[rows, width + at + n : 2 * width + at + n] = moved

    for r in range(groups):
        for f in range(2):
            at = chans + f * part
            place(f, r * cells, got_ref[r, at : at + part, :])

    even_ref[...] = nn(key_ref[...], qt_ref[:, 0:cells])
    chunk = total // 4

    def attend(r, now_ref, later_ref):
        later = jnp.minimum(r + 1, groups - 1)
        at = pl.ds(pl.multiple_of(r * cells, cells), cells)
        later = pl.ds(pl.multiple_of(later * cells, cells), cells)
        top = jnp.max(now_ref[...], 0, keepdims=True)
        count = jnp.zeros((1, cells), F32)
        for b in range(4):
            rows = slice(b * chunk, (b + 1) * chunk)
            later_ref[rows] = nn(key_ref[rows], qt_ref[:, later])
            raised = jnp.exp2((now_ref[rows] - top) * (scale * LOG2E))
            count = count + jnp.sum(raised, 0, keepdims=True)
            raised_ref[rows] = raised.astype(BF16)
        inv = 1.0 / count
        att = nn(vt_ref[...], raised_ref[...]) * inv
        att_ref[:, at] = att
        keep_att(r).start()
        top_ref[:, at] = top
        inv_ref[:, at] = inv

    def attend_two(n, carry):
        attend(2 * n, even_ref, odd_ref)
        attend(2 * n + 1, odd_ref, even_ref)
        return carry

    lax.fori_loop(0, groups // 2, attend_two, 0)
    for r in range(groups):
        x_pick = nt(pick_ref[...], x_ref[r])
        att = att_ref[:, r * cells : (r + 1) * cells].astype(BF16)
        place(2, r * cells, (x_pick + nn(wo_pick_ref[...], att)).astype(BF16))

    lane_tiles = chans // 128
    acc_ref[:, 27 * part :, :] = jnp.zeros((lane_tiles, 5 * part, 128), F32)
    for i in range(3):
        block = nt(side_ref[:, i * width : i * width + total], ut_ref[...])
        for t in range(3):
            for j in range(3):
                tap, at = 9 * t + 3 * i + j, (3 * t + j) * part
                for c in range(lane_tiles):
                    acc_ref[c, tap * part : (tap + 1) * part, :] = block[
                        at : at + part, c * 128 : (c + 1) * 128
                    ]
    near = give_ref.shape[0]
    for core, to_ref in ((1 - place_ref[1], give_ref), (place_ref[1], keep_ref)):
        for n in range(near):
            first = (n % 4) * 4 + (n // 4) * 2 + core
            for k in range(part // (2 * near)):
                for c in range(lane_tiles):
                    rows = acc_ref[c, pl.ds(k * 2 * near + first, 32, stride=part), :]
                    to_ref[n, k * 32 : (k + 1) * 32, c * 128 : (c + 1) * 128] = rows.astype(BF16)
    for copy in keeps:
        copy.wait()
    for r in range(groups):
        keep_att(r).wait()


def features_kernel(x_ref, gq_ref, gk_ref, gv_ref, gb_ref, wq_ref, wk_ref, wv_ref, out_ref):
    cells, chans = x_ref.shape
    x = nt(eye_of(chans), x_ref[...])
    recip = lax.rsqrt(jnp.mean(x * x, 0, keepdims=True) + 1e-06)
    grad_normed = (
        nn(wq_ref[...], gq_ref[...]) + nn(wk_ref[...], gk_ref[...]) + nn(wv_ref[...], gv_ref[...])
    )
    inner = jnp.mean(grad_normed * x, 0, keepdims=True)
    out = gb_ref[...].astype(F32) + recip * grad_normed - x * (recip * recip * recip) * inner
    out_ref[...] = nt(eye_of(cells), out.astype(BF16)).astype(BF16)


def backward_kernel(
    place_ref,
    x_ref,
    grad_in,
    qt_in,
    kt_in,
    key_in,
    value_in,
    att_in,
    top_ref,
    inv_ref,
    wo_order_ref,
    back_ref,
    gq_ref,
    gk_ref,
    gv_ref,
    gb_ref,
    give_ref,
    keep_ref,
    grad_ref,
    qt_ref,
    kt_ref,
    key_ref,
    value_ref,
    att_ref,
    term_ref,
    line_ref,
    sems,
    ga_ref,
    tot_ref,
    sq_ref,
    sk_ref,
    pb_ref,
    pq_ref,
    pk_ref,
):
    cells = x_ref.shape[0]
    chans, total = qt_ref.shape
    moves = [
        (key_in, key_ref),
        (qt_in, qt_ref),
        (grad_in, grad_ref),
        (att_in, att_ref),
        (value_in, value_ref),
        (kt_in, kt_ref),
    ]
    moves = [pltpu.make_async_copy(a, b, sems.at[n]) for n, (a, b) in enumerate(moves)]
    for copy in moves:
        copy.start()
    scale = chans ** (-0.5)
    mine = pl.ds(pl.multiple_of(place_ref[0] * cells, cells), cells)
    core = place_ref[1]
    chunk = total // 4
    chunks = [slice(b * chunk, (b + 1) * chunk) for b in range(4)]

    def probs_of(scores, top, inv):
        return jnp.exp2((scores - top) * (scale * LOG2E)) * inv

    for copy in moves[0:2]:
        copy.wait()
    key_mine = key_ref[mine, :]
    q_mine = qt_ref[:, mine]
    top_mine = top_ref[:, mine]
    inv_mine = inv_ref[:, mine]
    for at in chunks:
        pq_ref[at, :] = probs_of(nn(key_ref[at, :], q_mine), top_mine, inv_mine)
        pk_ref[:, at] = probs_of(nn(key_mine, qt_ref[:, at]), top_ref[:, at], inv_ref[:, at])
    for copy in moves[2:4]:
        copy.wait()
    for at in chunks:
        ga = nn(wo_order_ref[...], grad_ref[:, at]).astype(BF16)
        ga_ref[:, at] = ga
        tot_ref[:, at] = jnp.sum(att_ref[:, at] * ga.astype(F32), 0, keepdims=True)
    moves[4].wait()
    value_mine = value_ref[mine, :]
    ga_mine = ga_ref[:, mine]
    tot_mine = tot_ref[:, mine]
    for at in chunks:
        grad_probs = nn(value_ref[at, :], ga_mine)
        sq_ref[at, :] = (pq_ref[at, :] * (grad_probs - tot_mine) * scale).astype(BF16)
        probs = pk_ref[:, at]
        grad_probs = nn(value_mine, ga_ref[:, at])
        pb_ref[:, at] = probs.astype(BF16)
        sk_ref[:, at] = (probs * (grad_probs - tot_ref[:, at]) * scale).astype(BF16)

    moves[5].wait()
    gq = nn(kt_ref[...], sq_ref[...]).astype(BF16)
    gk = nt(qt_ref[...], sk_ref[...]).astype(BF16)
    gv = nt(ga_ref[...], pb_ref[...]).astype(BF16)
    gq_ref[...] = gq
    gk_ref[...] = gk
    gv_ref[...] = gv
    x = nt(eye_of(chans), x_ref[...])
    recip = lax.rsqrt(jnp.mean(x * x, 0, keepdims=True) + 1e-06)
    normed = (x * recip).astype(BF16)
    grad_b = nn(back_ref[...], grad_ref[:, mine])
    gb_ref[...] = grad_b.astype(BF16)
    att = att_ref[:, mine].astype(BF16)
    lane_tiles = chans // 128
    pairs = ((normed, gq), (normed, gk), (normed, gv), (att, grad_b.astype(BF16)))
    for n, (left, right) in enumerate(pairs):
        term = nt(left, right)
        for c in range(lane_tiles):
            term_ref[n * lane_tiles + c] = term[:, c * 128 : (c + 1) * 128]
    line_ref[...] = jnp.zeros(line_ref.shape, F32)
    groups = total // cells
    places = give_ref.shape[0] // (8 * groups)
    per = chans // (2 * places * groups)
    for half, to_ref in ((1 - core, give_ref), (core, keep_ref)):
        for place in range(places):
            for k in range(per):
                first = (2 * place + half) * per * groups + k
                for n in range(4):
                    to = pl.ds(place * groups * 8 + (n // 2) * 4 + k, groups, stride=8)
                    for c in range(lane_tiles):
                        rows = term_ref[n * lane_tiles + c, pl.ds(first, groups, stride=per), :]
                        line_ref[(n % 2) * lane_tiles + c, to, :] = rows
        for c in range(2 * lane_tiles):
            to_ref[:, c * 128 : (c + 1) * 128] = line_ref[c].astype(BF16)


def shards(
    features, past_frames, upstream, query_weight, key_weight, value_weight, out_weight, conv_weight
):
    slots, groups = lax.axis_size("dp"), lax.axis_size("rows")
    _, _, rows_here, width, chans = features.shape
    cells = rows_here * width
    total = cells * groups
    part = chans // groups
    per = part // slots
    me = lax.axis_index("rows")

    order = np.zeros((chans, chans), np.float32)
    for r in range(groups):
        for k in range(per):
            for d in range(slots):
                order[r * part + k * slots + d, d * per * groups + per * r + k] = 1.0
    order_b = jnp.asarray(order, BF16)
    back_b = jnp.asarray(order.T, BF16)

    pairs = slots // 2
    core = lax.rem(lax.axis_index("dp"), 2)

    x = features.reshape(cells, chans)
    u = upstream.reshape(cells, chans)
    past = past_frames.reshape(2, cells, chans)
    def across(block):
        return lax.ppermute(block, "rows", [(r, r ^ 1) for r in range(groups)])

    def along(block, step):
        return lax.ppermute(block, "rows", [(r, (r + 2 * step) % groups) for r in range(groups)])

    x_across = across(x)
    x_low, x_high = along(x, 1), along(x, -1)

    packed, w_local = pl.pallas_call(
        pack_kernel,
        out_shape=(
            jax.ShapeDtypeStruct((groups, chans + 2 * part, cells), BF16),
            jax.ShapeDtypeStruct((per, 16, chans), BF16),
        ),
        in_specs=whole(4),
        out_specs=tuple(whole(2)),
        compiler_params=params(56),
        name="pack",
    )(u, past, order_b, conv_weight)

    w_near = w_local.reshape(1, per * 16, chans)
    w_across = lax.ppermute(w_near, "dp", [(d, d ^ 2) for d in range(slots)])
    packed, w_across, x_across, x_low, x_high, place = lax.optimization_barrier(
        (packed, w_across, x_across, x_low, x_high, me.reshape(1))
    )
    x_low_across, x_high_across = along(x_across, 1), along(x_across, -1)
    x_far, x_far_across = along(x_low, 1), along(x_high_across, -1)
    x_all = (x, x_across, x_low, x_low_across, x_high, x_high_across, x_far, x_far_across)
    got = lax.all_to_all(packed, "rows", 0, 0)
    wqkv_t, wkv, pick, wo_pick, wo_order = pl.pallas_call(
        prepare_kernel,
        out_shape=(
            jax.ShapeDtypeStruct((3 * chans, chans), BF16),
            jax.ShapeDtypeStruct((chans, 2 * chans), BF16),
            jax.ShapeDtypeStruct((part, chans), BF16),
            jax.ShapeDtypeStruct((part, chans), BF16),
            jax.ShapeDtypeStruct((chans, chans), BF16),
        ),
        in_specs=[pl.BlockSpec(memory_space=pltpu.SMEM)] + whole(5),
        out_specs=tuple(whole(5)),
        compiler_params=params(56),
        name="prepare",
    )(place, query_weight, key_weight, value_weight, out_weight, order_b)

    w_across, wo_order = lax.optimization_barrier((w_across, wo_order))
    w_near = jnp.concatenate([w_near, w_across], 0)
    w_line = [w_near]
    for back in (1, 2, 3):
        w_line.append(lax.ppermute(w_near, "dp", [(d, (d + 4 * back) % slots) for d in range(slots)]))
    w_mine = jnp.concatenate(w_line, 0)
    w_other = lax.ppermute(w_mine, "dp", [(d, d ^ 1) for d in range(slots)])

    grad_sent = pl.pallas_call(
        lambda *refs: conv_input_kernel(width, *refs),
        out_shape=jax.ShapeDtypeStruct((groups, part, total), BF16),
        in_specs=[pl.BlockSpec(memory_space=pltpu.SMEM)] + whole(3),
        out_specs=in_hbm(1)[0],
        scratch_shapes=[
            pltpu.VMEM((9 * part, total + 2 * width), F32),
            pltpu.VMEM((chans // 128, slots * per * 16, 128), F32),
            pltpu.VMEM((9 * part, chans), BF16),
            pltpu.VMEM((part, total), BF16),
            pltpu.SemaphoreType.DMA((groups,)),
        ],
        compiler_params=params(56),
        name="conv_input",
    )(lax.axis_index("dp").reshape(1), got, w_mine, w_other)
    grad_sent, x_all = lax.optimization_barrier((grad_sent, x_all))
    grad_all = lax.all_to_all(grad_sent, "rows", 0, 0).reshape(chans, total)

    qt, kt, key, value, att, top, inv, conv_give, conv_keep = pl.pallas_call(
        lambda *refs: forward_kernel(width, *refs),
        out_shape=(
            jax.ShapeDtypeStruct((chans, total), BF16),
            jax.ShapeDtypeStruct((chans, total), BF16),
            jax.ShapeDtypeStruct((total, chans), BF16),
            jax.ShapeDtypeStruct((total, chans), BF16),
            jax.ShapeDtypeStruct((chans, total), F32),
            jax.ShapeDtypeStruct((1, total), F32),
            jax.ShapeDtypeStruct((1, total), F32),
            jax.ShapeDtypeStruct((slots // 2, per * 32, chans), BF16),
            jax.ShapeDtypeStruct((slots // 2, per * 32, chans), BF16),
        ),
        in_specs=[pl.BlockSpec(memory_space=pltpu.SMEM)] + anywhere(9) + whole(4),
        out_specs=tuple(anywhere(5) + whole(4)),
        scratch_shapes=[
            pltpu.VMEM(got.shape, BF16),
            pltpu.VMEM((groups, cells, chans), BF16),
            pltpu.VMEM((chans, total), BF16),
            pltpu.VMEM((chans, total), BF16),
            pltpu.VMEM((total, chans), BF16),
            pltpu.VMEM((total, chans), BF16),
            pltpu.VMEM((chans, total), F32),
            pltpu.SemaphoreType.DMA((groups,)),
            pltpu.SemaphoreType.DMA((groups,)),
            pltpu.SemaphoreType.DMA((4,)),
            pltpu.SemaphoreType.DMA((groups,)),
            pltpu.VMEM((chans, total), BF16),
            pltpu.VMEM((9 * part, total + 2 * width), BF16),
            pltpu.VMEM((chans, total), BF16),
            pltpu.VMEM((chans // 128, 32 * part, 128), F32),
            pltpu.VMEM((total, cells), F32),
            pltpu.VMEM((total, cells), F32),
            pltpu.VMEM((total, cells), BF16),
        ],
        compiler_params=params(56),
        name="forward",
    )(jnp.stack([me, core]), got, *x_all, wqkv_t, wkv, pick, wo_pick)
    conv_taken = lax.ppermute(conv_give, "dp", [(d, d ^ 1) for d in range(slots)])

    gq, gk, gv, gb, give, keep = pl.pallas_call(
        backward_kernel,
        out_shape=(
            jax.ShapeDtypeStruct((chans, cells), BF16),
            jax.ShapeDtypeStruct((chans, cells), BF16),
            jax.ShapeDtypeStruct((chans, cells), BF16),
            jax.ShapeDtypeStruct((chans, cells), BF16),
            jax.ShapeDtypeStruct((pairs * groups * 8, 2 * chans), BF16),
            jax.ShapeDtypeStruct((pairs * groups * 8, 2 * chans), BF16),
        ),
        in_specs=[pl.BlockSpec(memory_space=pltpu.SMEM)] + whole(1) + anywhere(6) + whole(4),
        out_specs=tuple(whole(6)),
        scratch_shapes=[
            pltpu.VMEM((chans, total), BF16),
            pltpu.VMEM((chans, total), BF16),
            pltpu.VMEM((chans, total), BF16),
            pltpu.VMEM((total, chans), BF16),
            pltpu.VMEM((total, chans), BF16),
            pltpu.VMEM((chans, total), F32),
            pltpu.VMEM((4 * chans // 128, chans, 128), F32),
            pltpu.VMEM((2 * chans // 128, pairs * groups * 8, 128), F32),
            pltpu.SemaphoreType.DMA((6,)),
            pltpu.VMEM((chans, total), BF16),
            pltpu.VMEM((1, total), F32),
            pltpu.VMEM((total, cells), BF16),
            pltpu.VMEM((cells, total), BF16),
            pltpu.VMEM((cells, total), BF16),
            pltpu.VMEM((total, cells), F32),
            pltpu.VMEM((cells, total), F32),
        ],
        compiler_params=params(56),
        name="backward",
    )(
        jnp.stack([me, core]),
        x,
        grad_all,
        qt,
        kt,
        key,
        value,
        att,
        top,
        inv,
        wo_order,
        back_b,
    )

    taken = lax.ppermute(give, "dp", [(d, d ^ 1) for d in range(slots)])
    chip = (keep.astype(F32) + taken.astype(F32)).astype(BF16)
    chip = chip.reshape(pairs * groups, 8, 2 * chans)
    same_core = [[d * groups + r for d in range(c, slots, 2) for r in range(groups)] for c in range(2)]
    conv_taken, chip, gb = lax.optimization_barrier((conv_taken, chip, gb))
    got_chip = lax.all_to_all(chip, ("dp", "rows"), 0, 0, axis_index_groups=same_core)
    feature_grad = pl.pallas_call(
        features_kernel,
        out_shape=jax.ShapeDtypeStruct((cells, chans), BF16),
        in_specs=whole(8),
        out_specs=pl.BlockSpec(memory_space=pltpu.VMEM),
        compiler_params=params(56),
        name="features",
    )(x, gq, gk, gv, gb, query_weight, key_weight, value_weight)
    me_dp = lax.axis_index("dp")
    z, y = lax.div(me_dp, 4), lax.rem(lax.div(me_dp, 2), 2)
    conv_line = conv_keep.astype(F32) + conv_taken.astype(F32)
    sent = lax.dynamic_slice_in_dim(conv_line, (1 - y) * 4, 4, 0).astype(BF16)
    taken = lax.ppermute(sent, "dp", [(d, d ^ 2) for d in range(slots)])
    conv_line = lax.dynamic_slice_in_dim(conv_line, y * 4, 4, 0) + taken.astype(F32)
    conv_sum = lax.dynamic_index_in_dim(conv_line, z, 0, keepdims=False)
    for on in (1, 2, 3):
        sent = lax.dynamic_index_in_dim(conv_line, lax.rem(z + on, 4), 0, keepdims=False).astype(BF16)
        taken = lax.ppermute(sent, "dp", [(d, (d + 4 * on) % slots) for d in range(slots)])
        conv_sum = conv_sum + taken.astype(F32)
    conv_grad = conv_sum.reshape(per, 32, chans)[:, :27].reshape(per, 27 * chans)
    proj = jnp.sum(got_chip.astype(F32), 0).reshape(2, 4, 2, chans)[:, :per]
    proj_grads = proj.transpose(1, 0, 2, 3).reshape(per, 4 * chans)
    return feature_grad.reshape(features.shape), proj_grads, conv_grad


def solution(mesh):
    placed = (
        P("dp", None, "rows", None, None),
        P("dp", None, "rows", None, None),
        P("dp", None, "rows", None, None),
        P(),
        P(),
        P(),
        P(),
        P(("dp", "rows"), None, None),
    )
    return jax.shard_map(
        shards,
        mesh=mesh,
        in_specs=placed,
        out_specs=(
            P("dp", None, "rows", None, None),
            P(("dp", "rows"), None),
            P(("dp", "rows"), None),
        ),
        check_vma=False,
    )
```

```python
import jax
import jax.numpy as jnp
import numpy as np
from jax import lax
from jax.experimental import pallas as pl
from jax.experimental.pallas import tpu as pltpu
from jax.sharding import PartitionSpec as P

F32 = jnp.float32
BF16 = jnp.bfloat16
LOG2E = 1.4426950408889634


def nn(a, b):
    return lax.dot_general(a, b, (((1,), (0,)), ((), ())), preferred_element_type=F32)


def nt(a, b):
    return lax.dot_general(a, b, (((1,), (1,)), ((), ())), preferred_element_type=F32)


def whole(count):
    return [pl.BlockSpec(memory_space=pltpu.VMEM)] * count


def anywhere(count):
    return [pl.BlockSpec(memory_space=pl.ANY)] * count


def in_hbm(count):
    return [pl.BlockSpec(memory_space=pltpu.HBM)] * count


def params(mib):
    return pltpu.CompilerParams(vmem_limit_bytes=mib * 1024 * 1024)


def cost(macs, size):
    return pl.CostEstimate(flops=2 * macs, bytes_accessed=size, transcendentals=0)


def eye_of(n):
    rows = lax.broadcasted_iota(jnp.int32, (n, n), 0)
    cols = lax.broadcasted_iota(jnp.int32, (n, n), 1)
    return jnp.where(rows == cols, 1.0, 0.0).astype(BF16)


def pack_kernel(u_ref, past_ref, order_ref, conv_ref, out_ref, w_ref):
    chans = u_ref.shape[1]
    groups = out_ref.shape[0]
    part = chans // groups
    w_ref[...] = jnp.zeros(w_ref.shape, BF16)
    for k in range(w_ref.shape[0]):
        w_ref[k, 0:11, :] = conv_ref[k, 16:27, :]
    u_t = nt(eye_of(chans), u_ref[...]).astype(BF16)
    for r in range(groups):
        out_ref[r, 0:chans, :] = u_t
    for f in range(2):
        p_t = nt(order_ref[...], past_ref[f]).astype(BF16)
        for r in range(groups):
            at = chans + f * part
            out_ref[r, at : at + part, :] = p_t[r * part : (r + 1) * part]


def prepare_kernel(me_ref, wq_ref, wk_ref, wv_ref, wo_ref, order_ref, wqkv_t_ref, wkv_ref, pick_ref, wo_pick_ref, wo_order_ref):
    chans = wq_ref.shape[0]
    part = pick_ref.shape[0]
    eye = eye_of(chans)
    for n, ref in enumerate((wq_ref, wk_ref, wv_ref)):
        wqkv_t_ref[n * chans : (n + 1) * chans, :] = nt(eye, ref[...]).astype(BF16)
    wkv_ref[:, 0:chans] = wk_ref[...]
    wkv_ref[:, chans:] = wv_ref[...]
    pick = order_ref[pl.ds(pl.multiple_of(me_ref[0] * part, part), part), :]
    pick_ref[...] = pick
    wo_pick_ref[...] = nn(pick, nt(eye, wo_ref[...]).astype(BF16)).astype(BF16)
    wo_order_ref[...] = nt(wo_ref[...], order_ref[...]).astype(BF16)


def conv_input_kernel(width, me_ref, got_ref, w_mine_ref, w_other_ref, *refs):
    out_ref, wide_ref, w32_ref, wcat_ref, grad_ref, sems = refs[-6:]
    groups = got_ref.shape[0]
    cells = got_ref.shape[2]
    part, total = out_ref.shape[1:]
    near, padded, chans = w_mine_ref.shape
    slots = 2 * near
    per = part // slots
    z, y, core = lax.div(me_ref[0], 4), lax.rem(lax.div(me_ref[0], 2), 2), lax.rem(me_ref[0], 2)
    for apart, w_ref in enumerate((w_mine_ref, w_other_ref)):
        for n in range(near):
            at = lax.rem(z + 4 - n // 2, 4) * 4 + lax.rem(y + n % 2, 2) * 2 + lax.rem(core + apart, 2)
            at = pl.ds(pl.multiple_of(at * padded, padded), padded)
            for c in range(chans // 128):
                w32_ref[c, at, :] = w_ref[n, :, c * 128 : (c + 1) * 128].astype(F32)
    for c in range(chans // 128):
        lanes = slice(c * 128, (c + 1) * 128)
        for tap in range(9):
            for k in range(per):
                rows = w32_ref[c, pl.ds(k * 16 + 2 + tap, slots, stride=padded), :]
                at = tap * part + k * slots
                wcat_ref[at : at + slots, lanes] = rows.astype(BF16)
    wide_ref[:, 0:width] = jnp.zeros((9 * part, width), F32)
    wide_ref[:, width + total :] = jnp.zeros((9 * part, width), F32)
    for r in range(groups):
        wide_ref[:, width + r * cells : width + (r + 1) * cells] = nn(
            wcat_ref[...], got_ref[r, 0:chans, :]
        )
    lane = lax.broadcasted_iota(jnp.int32, (part, total), 1) % width
    sums = []
    for j in range(3):
        piece = None
        for i in range(3):
            tap = 3 * i + j
            at = (2 - i) * width
            term = wide_ref[tap * part : (tap + 1) * part, at : at + total]
            piece = term if piece is None else piece + term
        sums.append(piece)
    first = jnp.where(lane == width - 1, 0.0, pltpu.roll(sums[0], total - 1, 1))
    last = jnp.where(lane == 0, 0.0, pltpu.roll(sums[2], 1, 1))
    grad_ref[...] = (first + sums[1] + last).astype(BF16)
    copies = [pltpu.make_async_copy(grad_ref, out_ref.at[r], sems.at[r]) for r in range(groups)]
    for copy in copies:
        copy.start()
    for copy in copies:
        copy.wait()


def forward_kernel(
    width,
    place_ref,
    got_in,
    x0_in,
    x1_in,
    x2_in,
    x3_in,
    x4_in,
    x5_in,
    x6_in,
    x7_in,
    wqkv_t_ref,
    wkv_ref,
    pick_ref,
    wo_pick_ref,
    qt_out,
    kt_out,
    key_out,
    value_out,
    att_out,
    top_ref,
    inv_ref,
    give_ref,
    keep_ref,
    got_ref,
    x_ref,
    qt_ref,
    kt_ref,
    key_ref,
    value_ref,
    att_ref,
    in_sems,
    x_sems,
    out_sems,
    att_sems,
    vt_ref,
    side_ref,
    ut_ref,
    acc_ref,
    even_ref,
    odd_ref,
    raised_ref,
):
    groups, cells = got_ref.shape[0], got_ref.shape[2]
    chans = wkv_ref.shape[0]
    total = groups * cells
    part = chans // groups

    me = place_ref[0]
    fetches = []
    for n, ref in enumerate((x0_in, x1_in, x2_in, x3_in, x4_in, x5_in, x6_in, x7_in)):
        plane = lax.rem(lax.div(me, 2) + (0, 3, 1, 2)[n // 2], 4)
        at = plane * 2 + lax.rem(me + n % 2, 2)
        fetches.append(pltpu.make_async_copy(ref, x_ref.at[at], x_sems.at[n]))
    for r in range(groups):
        fetches.append(pltpu.make_async_copy(got_in.at[r], got_ref.at[r], in_sems.at[r]))
    for fetch in fetches:
        fetch.start()
    kept = [(qt_ref, qt_out), (kt_ref, kt_out), (key_ref, key_out), (value_ref, value_out)]
    keeps = [pltpu.make_async_copy(a, b, out_sems.at[n]) for n, (a, b) in enumerate(kept)]

    def keep_att(r):
        at = pl.ds(pl.multiple_of(r * cells, cells), cells)
        return pltpu.make_async_copy(att_ref.at[:, at], att_out.at[:, at], att_sems.at[r])

    scale = chans ** (-0.5)
    def project(r, carry):
        x = x_ref[r].astype(F32)
        recip = lax.rsqrt(jnp.mean(x * x, 1, keepdims=True) + 1e-06)
        normed = (x * recip).astype(BF16)
        at = pl.ds(pl.multiple_of(r * cells, cells), cells)
        qkv_t = nt(wqkv_t_ref[...], normed).astype(BF16)
        qt_ref[:, at] = qkv_t[0:chans]
        kt_ref[:, at] = qkv_t[chans : 2 * chans]
        vt_ref[:, at] = qkv_t[2 * chans :]
        kv = nn(normed, wkv_ref[...]).astype(BF16)
        key_ref[at, :] = kv[:, 0:chans]
        value_ref[at, :] = kv[:, chans:]
        return carry

    for fetch in fetches[:groups]:
        fetch.wait()
    lax.fori_loop(0, groups, project, 0, unroll=2)
    for fetch in fetches[groups:]:
        fetch.wait()
    for copy in keeps:
        copy.start()
    for r in range(groups):
        ut_ref[:, r * cells : (r + 1) * cells] = got_ref[r, 0:chans, :]

    for n in range(9):
        rows = slice(n * part, (n + 1) * part)
        side_ref[rows, 0:width] = jnp.zeros((part, width), BF16)
        side_ref[rows, width + total :] = jnp.zeros((part, width), BF16)

    lane = lax.broadcasted_iota(jnp.int32, (part, width), 1)

    def place(t, at, block):
        for n in range(0, cells, width):
            one = block[:, n : n + width]
            one32 = one.astype(F32)
            left = jnp.where(lane == 0, 0.0, pltpu.roll(one32, 1, 1))
            right = jnp.where(lane == width - 1, 0.0, pltpu.roll(one32, width - 1, 1))
            for j, moved in enumerate((left.astype(BF16), one, right.astype(BF16))):
                rows = slice((3 * t + j) * part, (3 * t + j + 1) * part)
                side_ref[rows, width + at + n : 2 * width + at + n] = moved

    for r in range(groups):
        for f in range(2):
            at = chans + f * part
            place(f, r * cells, got_ref[r, at : at + part, :])

    even_ref[...] = nn(key_ref[...], qt_ref[:, 0:cells])
    chunk = total // 4

    def attend(r, now_ref, later_ref):
        later = jnp.minimum(r + 1, groups - 1)
        at = pl.ds(pl.multiple_of(r * cells, cells), cells)
        later = pl.ds(pl.multiple_of(later * cells, cells), cells)
        top = jnp.max(now_ref[...], 0, keepdims=True)
        count = jnp.zeros((1, cells), F32)
        for b in range(4):
            rows = slice(b * chunk, (b + 1) * chunk)
            later_ref[rows] = nn(key_ref[rows], qt_ref[:, later])
            raised = jnp.exp2((now_ref[rows] - top) * (scale * LOG2E))
            count = count + jnp.sum(raised, 0, keepdims=True)
            raised_ref[rows] = raised.astype(BF16)
        inv = 1.0 / count
        att = nn(vt_ref[...], raised_ref[...]) * inv
        att_ref[:, at] = att
        keep_att(r).start()
        top_ref[:, at] = top
        inv_ref[:, at] = inv

    def attend_two(n, carry):
        attend(2 * n, even_ref, odd_ref)
        attend(2 * n + 1, odd_ref, even_ref)
        return carry

    lax.fori_loop(0, groups // 2, attend_two, 0)
    for r in range(groups):
        x_pick = nt(pick_ref[...], x_ref[r])
        att = att_ref[:, r * cells : (r + 1) * cells].astype(BF16)
        place(2, r * cells, (x_pick + nn(wo_pick_ref[...], att)).astype(BF16))

    lane_tiles = chans // 128
    acc_ref[:, 27 * part :, :] = jnp.zeros((lane_tiles, 5 * part, 128), F32)
    for i in range(3):
        block = nt(side_ref[:, i * width : i * width + total], ut_ref[...])
        for t in range(3):
            for j in range(3):
                tap, at = 9 * t + 3 * i + j, (3 * t + j) * part
                for c in range(lane_tiles):
                    acc_ref[c, tap * part : (tap + 1) * part, :] = block[
                        at : at + part, c * 128 : (c + 1) * 128
                    ]
    near = give_ref.shape[0]
    for core, to_ref in ((1 - place_ref[1], give_ref), (place_ref[1], keep_ref)):
        for n in range(near):
            first = (n % 4) * 4 + (n // 4) * 2 + core
            for k in range(part // (2 * near)):
                for c in range(lane_tiles):
                    rows = acc_ref[c, pl.ds(k * 2 * near + first, 32, stride=part), :]
                    to_ref[n, k * 32 : (k + 1) * 32, c * 128 : (c + 1) * 128] = rows.astype(BF16)
    for copy in keeps:
        copy.wait()
    for r in range(groups):
        keep_att(r).wait()


def features_kernel(x_ref, gq_ref, gk_ref, gv_ref, gb_ref, wq_ref, wk_ref, wv_ref, out_ref):
    cells, chans = x_ref.shape
    x = nt(eye_of(chans), x_ref[...])
    recip = lax.rsqrt(jnp.mean(x * x, 0, keepdims=True) + 1e-06)
    grad_normed = (
        nn(wq_ref[...], gq_ref[...]) + nn(wk_ref[...], gk_ref[...]) + nn(wv_ref[...], gv_ref[...])
    )
    inner = jnp.mean(grad_normed * x, 0, keepdims=True)
    out = gb_ref[...].astype(F32) + recip * grad_normed - x * (recip * recip * recip) * inner
    out_ref[...] = nt(eye_of(cells), out.astype(BF16)).astype(BF16)


def backward_kernel(
    place_ref,
    x_ref,
    grad_in,
    qt_in,
    kt_in,
    key_in,
    value_in,
    att_in,
    top_ref,
    inv_ref,
    wo_order_ref,
    back_ref,
    gq_ref,
    gk_ref,
    gv_ref,
    gb_ref,
    give_ref,
    keep_ref,
    grad_ref,
    qt_ref,
    kt_ref,
    key_ref,
    value_ref,
    att_ref,
    term_ref,
    line_ref,
    sems,
    ga_ref,
    tot_ref,
    sq_ref,
    sk_ref,
    pb_ref,
    pq_ref,
    pk_ref,
):
    cells = x_ref.shape[0]
    chans, total = qt_ref.shape
    moves = [
        (key_in, key_ref),
        (qt_in, qt_ref),
        (grad_in, grad_ref),
        (att_in, att_ref),
        (value_in, value_ref),
        (kt_in, kt_ref),
    ]
    moves = [pltpu.make_async_copy(a, b, sems.at[n]) for n, (a, b) in enumerate(moves)]
    for copy in moves:
        copy.start()
    scale = chans ** (-0.5)
    mine = pl.ds(pl.multiple_of(place_ref[0] * cells, cells), cells)
    core = place_ref[1]
    chunk = total // 4
    chunks = [slice(b * chunk, (b + 1) * chunk) for b in range(4)]

    def probs_of(scores, top, inv):
        return jnp.exp2((scores - top) * (scale * LOG2E)) * inv

    for copy in moves[0:2]:
        copy.wait()
    key_mine = key_ref[mine, :]
    q_mine = qt_ref[:, mine]
    top_mine = top_ref[:, mine]
    inv_mine = inv_ref[:, mine]
    for at in chunks:
        pq_ref[at, :] = probs_of(nn(key_ref[at, :], q_mine), top_mine, inv_mine)
        pk_ref[:, at] = probs_of(nn(key_mine, qt_ref[:, at]), top_ref[:, at], inv_ref[:, at])
    for copy in moves[2:4]:
        copy.wait()
    for at in chunks:
        ga = nn(wo_order_ref[...], grad_ref[:, at]).astype(BF16)
        ga_ref[:, at] = ga
        tot_ref[:, at] = jnp.sum(att_ref[:, at] * ga.astype(F32), 0, keepdims=True)
    moves[4].wait()
    value_mine = value_ref[mine, :]
    ga_mine = ga_ref[:, mine]
    tot_mine = tot_ref[:, mine]
    for at in chunks:
        grad_probs = nn(value_ref[at, :], ga_mine)
        sq_ref[at, :] = (pq_ref[at, :] * (grad_probs - tot_mine) * scale).astype(BF16)
        probs = pk_ref[:, at]
        grad_probs = nn(value_mine, ga_ref[:, at])
        pb_ref[:, at] = probs.astype(BF16)
        sk_ref[:, at] = (probs * (grad_probs - tot_ref[:, at]) * scale).astype(BF16)

    moves[5].wait()
    gq = nn(kt_ref[...], sq_ref[...]).astype(BF16)
    gk = nt(qt_ref[...], sk_ref[...]).astype(BF16)
    gv = nt(ga_ref[...], pb_ref[...]).astype(BF16)
    gq_ref[...] = gq
    gk_ref[...] = gk
    gv_ref[...] = gv
    x = nt(eye_of(chans), x_ref[...])
    recip = lax.rsqrt(jnp.mean(x * x, 0, keepdims=True) + 1e-06)
    normed = (x * recip).astype(BF16)
    grad_b = nn(back_ref[...], grad_ref[:, mine])
    gb_ref[...] = grad_b.astype(BF16)
    att = att_ref[:, mine].astype(BF16)
    lane_tiles = chans // 128
    pairs = ((normed, gq), (normed, gk), (normed, gv), (att, grad_b.astype(BF16)))
    for n, (left, right) in enumerate(pairs):
        term = nt(left, right)
        for c in range(lane_tiles):
            term_ref[n * lane_tiles + c] = term[:, c * 128 : (c + 1) * 128]
    line_ref[...] = jnp.zeros(line_ref.shape, F32)
    groups = total // cells
    places = give_ref.shape[0] // (8 * groups)
    per = chans // (2 * places * groups)
    for half, to_ref in ((1 - core, give_ref), (core, keep_ref)):
        for place in range(places):
            for k in range(per):
                first = (2 * place + half) * per * groups + k
                for n in range(4):
                    to = pl.ds(place * groups * 8 + (n // 2) * 4 + k, groups, stride=8)
                    for c in range(lane_tiles):
                        rows = term_ref[n * lane_tiles + c, pl.ds(first, groups, stride=per), :]
                        line_ref[(n % 2) * lane_tiles + c, to, :] = rows
        for c in range(2 * lane_tiles):
            to_ref[:, c * 128 : (c + 1) * 128] = line_ref[c].astype(BF16)


def add_kernel(one_ref, other_ref, out_ref):
    out_ref[...] = (one_ref[...].astype(F32) + other_ref[...].astype(F32)).astype(BF16)


def shards(
    features, past_frames, upstream, query_weight, key_weight, value_weight, out_weight, conv_weight
):
    slots, groups = lax.axis_size("dp"), lax.axis_size("rows")
    _, _, rows_here, width, chans = features.shape
    cells = rows_here * width
    total = cells * groups
    part = chans // groups
    per = part // slots
    me = lax.axis_index("rows")

    order = np.zeros((chans, chans), np.float32)
    for r in range(groups):
        for k in range(per):
            for d in range(slots):
                order[r * part + k * slots + d, d * per * groups + per * r + k] = 1.0
    order_b = jnp.asarray(order, BF16)
    back_b = jnp.asarray(order.T, BF16)

    pairs = slots // 2
    core = lax.rem(lax.axis_index("dp"), 2)

    x = features.reshape(cells, chans)
    u = upstream.reshape(cells, chans)
    past = past_frames.reshape(2, cells, chans)
    def across(block):
        return lax.ppermute(block, "rows", [(r, r ^ 1) for r in range(groups)])

    def along(block, step):
        return lax.ppermute(block, "rows", [(r, (r + 2 * step) % groups) for r in range(groups)])

    x_across = across(x)
    x_low, x_high = along(x, 1), along(x, -1)

    packed, w_local = pl.pallas_call(
        pack_kernel,
        out_shape=(
            jax.ShapeDtypeStruct((groups, chans + 2 * part, cells), BF16),
            jax.ShapeDtypeStruct((per, 16, chans), BF16),
        ),
        in_specs=whole(4),
        out_specs=tuple(whole(2)),
        compiler_params=params(56),
        name="pack",
    )(u, past, order_b, conv_weight)

    w_near = w_local.reshape(1, per * 16, chans)
    w_across = lax.ppermute(w_near, "dp", [(d, d ^ 2) for d in range(slots)])
    packed, w_across, x_across, x_low, x_high, place = lax.optimization_barrier(
        (packed, w_across, x_across, x_low, x_high, me.reshape(1))
    )
    x_low_across, x_high_across = along(x_across, 1), along(x_across, -1)
    x_far, x_far_across = along(x_low, 1), along(x_high_across, -1)
    x_all = (x, x_across, x_low, x_low_across, x_high, x_high_across, x_far, x_far_across)
    got = lax.all_to_all(packed, "rows", 0, 0)
    wqkv_t, wkv, pick, wo_pick, wo_order = pl.pallas_call(
        prepare_kernel,
        out_shape=(
            jax.ShapeDtypeStruct((3 * chans, chans), BF16),
            jax.ShapeDtypeStruct((chans, 2 * chans), BF16),
            jax.ShapeDtypeStruct((part, chans), BF16),
            jax.ShapeDtypeStruct((part, chans), BF16),
            jax.ShapeDtypeStruct((chans, chans), BF16),
        ),
        in_specs=[pl.BlockSpec(memory_space=pltpu.SMEM)] + whole(5),
        out_specs=tuple(whole(5)),
        compiler_params=params(56),
        name="prepare",
    )(place, query_weight, key_weight, value_weight, out_weight, order_b)

    w_across, wo_order = lax.optimization_barrier((w_across, wo_order))
    w_near = jnp.concatenate([w_near, w_across], 0)
    w_line = [w_near]
    for back in (1, 2, 3):
        w_line.append(lax.ppermute(w_near, "dp", [(d, (d + 4 * back) % slots) for d in range(slots)]))
    w_mine = jnp.concatenate(w_line, 0)
    w_other = lax.ppermute(w_mine, "dp", [(d, d ^ 1) for d in range(slots)])

    grad_sent = pl.pallas_call(
        lambda *refs: conv_input_kernel(width, *refs),
        out_shape=jax.ShapeDtypeStruct((groups, part, total), BF16),
        in_specs=[pl.BlockSpec(memory_space=pltpu.SMEM)] + whole(3),
        out_specs=in_hbm(1)[0],
        scratch_shapes=[
            pltpu.VMEM((9 * part, total + 2 * width), F32),
            pltpu.VMEM((chans // 128, slots * per * 16, 128), F32),
            pltpu.VMEM((9 * part, chans), BF16),
            pltpu.VMEM((part, total), BF16),
            pltpu.SemaphoreType.DMA((groups,)),
        ],
        compiler_params=params(56),
        name="conv_input",
    )(lax.axis_index("dp").reshape(1), got, w_mine, w_other)
    grad_sent, x_all = lax.optimization_barrier((grad_sent, x_all))
    grad_all = lax.all_to_all(grad_sent, "rows", 0, 0).reshape(chans, total)

    qt, kt, key, value, att, top, inv, conv_give, conv_keep = pl.pallas_call(
        lambda *refs: forward_kernel(width, *refs),
        out_shape=(
            jax.ShapeDtypeStruct((chans, total), BF16),
            jax.ShapeDtypeStruct((chans, total), BF16),
            jax.ShapeDtypeStruct((total, chans), BF16),
            jax.ShapeDtypeStruct((total, chans), BF16),
            jax.ShapeDtypeStruct((chans, total), F32),
            jax.ShapeDtypeStruct((1, total), F32),
            jax.ShapeDtypeStruct((1, total), F32),
            jax.ShapeDtypeStruct((slots // 2, per * 32, chans), BF16),
            jax.ShapeDtypeStruct((slots // 2, per * 32, chans), BF16),
        ),
        in_specs=[pl.BlockSpec(memory_space=pltpu.SMEM)] + anywhere(9) + whole(4),
        out_specs=tuple(anywhere(5) + whole(4)),
        scratch_shapes=[
            pltpu.VMEM(got.shape, BF16),
            pltpu.VMEM((groups, cells, chans), BF16),
            pltpu.VMEM((chans, total), BF16),
            pltpu.VMEM((chans, total), BF16),
            pltpu.VMEM((total, chans), BF16),
            pltpu.VMEM((total, chans), BF16),
            pltpu.VMEM((chans, total), F32),
            pltpu.SemaphoreType.DMA((groups,)),
            pltpu.SemaphoreType.DMA((groups,)),
            pltpu.SemaphoreType.DMA((4,)),
            pltpu.SemaphoreType.DMA((groups,)),
            pltpu.VMEM((chans, total), BF16),
            pltpu.VMEM((9 * part, total + 2 * width), BF16),
            pltpu.VMEM((chans, total), BF16),
            pltpu.VMEM((chans // 128, 32 * part, 128), F32),
            pltpu.VMEM((total, cells), F32),
            pltpu.VMEM((total, cells), F32),
            pltpu.VMEM((total, cells), BF16),
        ],
        compiler_params=params(56),
        name="forward",
    )(jnp.stack([me, core]), got, *x_all, wqkv_t, wkv, pick, wo_pick)
    conv_taken = lax.ppermute(conv_give, "dp", [(d, d ^ 1) for d in range(slots)])

    gq, gk, gv, gb, give, keep = pl.pallas_call(
        backward_kernel,
        out_shape=(
            jax.ShapeDtypeStruct((chans, cells), BF16),
            jax.ShapeDtypeStruct((chans, cells), BF16),
            jax.ShapeDtypeStruct((chans, cells), BF16),
            jax.ShapeDtypeStruct((chans, cells), BF16),
            jax.ShapeDtypeStruct((pairs * groups * 8, 2 * chans), BF16),
            jax.ShapeDtypeStruct((pairs * groups * 8, 2 * chans), BF16),
        ),
        in_specs=[pl.BlockSpec(memory_space=pltpu.SMEM)] + whole(1) + anywhere(6) + whole(4),
        out_specs=tuple(whole(6)),
        scratch_shapes=[
            pltpu.VMEM((chans, total), BF16),
            pltpu.VMEM((chans, total), BF16),
            pltpu.VMEM((chans, total), BF16),
            pltpu.VMEM((total, chans), BF16),
            pltpu.VMEM((total, chans), BF16),
            pltpu.VMEM((chans, total), F32),
            pltpu.VMEM((4 * chans // 128, chans, 128), F32),
            pltpu.VMEM((2 * chans // 128, pairs * groups * 8, 128), F32),
            pltpu.SemaphoreType.DMA((6,)),
            pltpu.VMEM((chans, total), BF16),
            pltpu.VMEM((1, total), F32),
            pltpu.VMEM((total, cells), BF16),
            pltpu.VMEM((cells, total), BF16),
            pltpu.VMEM((cells, total), BF16),
            pltpu.VMEM((total, cells), F32),
            pltpu.VMEM((cells, total), F32),
        ],
        compiler_params=params(56),
        name="backward",
    )(
        jnp.stack([me, core]),
        x,
        grad_all,
        qt,
        kt,
        key,
        value,
        att,
        top,
        inv,
        wo_order,
        back_b,
    )

    taken = lax.ppermute(give, "dp", [(d, d ^ 1) for d in range(slots)])
    chip = pl.pallas_call(
        add_kernel,
        out_shape=jax.ShapeDtypeStruct(keep.shape, BF16),
        in_specs=whole(2),
        out_specs=pl.BlockSpec(memory_space=pltpu.VMEM),
        compiler_params=params(56),
        name="add",
    )(keep, taken)
    chip = chip.reshape(pairs * groups, 8, 2 * chans)
    same_core = [[d * groups + r for d in range(c, slots, 2) for r in range(groups)] for c in range(2)]
    conv_taken, chip, gb = lax.optimization_barrier((conv_taken, chip, gb))
    got_chip = lax.all_to_all(chip, ("dp", "rows"), 0, 0, axis_index_groups=same_core)
    feature_grad = pl.pallas_call(
        features_kernel,
        out_shape=jax.ShapeDtypeStruct((cells, chans), BF16),
        in_specs=whole(8),
        out_specs=pl.BlockSpec(memory_space=pltpu.VMEM),
        compiler_params=params(56),
        name="features",
    )(x, gq, gk, gv, gb, query_weight, key_weight, value_weight)
    me_dp = lax.axis_index("dp")
    z, y = lax.div(me_dp, 4), lax.rem(lax.div(me_dp, 2), 2)
    conv_line = conv_keep.astype(F32) + conv_taken.astype(F32)
    sent = lax.dynamic_slice_in_dim(conv_line, (1 - y) * 4, 4, 0).astype(BF16)
    taken = lax.ppermute(sent, "dp", [(d, d ^ 2) for d in range(slots)])
    conv_line = lax.dynamic_slice_in_dim(conv_line, y * 4, 4, 0) + taken.astype(F32)
    conv_sum = lax.dynamic_index_in_dim(conv_line, z, 0, keepdims=False)
    for on in (1, 2, 3):
        sent = lax.dynamic_index_in_dim(conv_line, lax.rem(z + on, 4), 0, keepdims=False).astype(BF16)
        taken = lax.ppermute(sent, "dp", [(d, (d + 4 * on) % slots) for d in range(slots)])
        conv_sum = conv_sum + taken.astype(F32)
    conv_grad = conv_sum.reshape(per, 32, chans)[:, :27].reshape(per, 27 * chans)
    proj = jnp.sum(got_chip.astype(F32), 0).reshape(2, 4, 2, chans)[:, :per]
    proj_grads = proj.transpose(1, 0, 2, 3).reshape(per, 4 * chans)
    return feature_grad.reshape(features.shape), proj_grads, conv_grad


def solution(mesh):
    placed = (
        P("dp", None, "rows", None, None),
        P("dp", None, "rows", None, None),
        P("dp", None, "rows", None, None),
        P(),
        P(),
        P(),
        P(),
        P(("dp", "rows"), None, None),
    )
    return jax.shard_map(
        shards,
        mesh=mesh,
        in_specs=placed,
        out_specs=(
            P("dp", None, "rows", None, None),
            P(("dp", "rows"), None),
            P(("dp", "rows"), None),
        ),
        check_vma=False,
    )
```
